32 devices in a mesh: section: 2 (over core), seq: 4 (over z), chan: 4 (over y, x).
Axes of the slice: x: 2, y: 2, z: 4, core: 2. Of those that a mesh axis runs over, the one named last changes fastest.
Arguments:
- layer_inputs: bfloat16 [2, 4, 256, 4096], P('section', None, 'seq', 'chan')
- out_grad: bfloat16 [4, 256, 4096], P(None, 'seq', 'chan')
- rate_weight: bfloat16 [2, 16, 256, 256], P('section', 'chan'), may hold values from -0.375 to 0.375
- input_weight: bfloat16 [2, 16, 256, 256], P('section', 'chan'), may hold values from -0.375 to 0.375
- rate_bias: float32 [2, 4096], P('section', 'chan'), may hold values from -4 to 4
- input_bias: float32 [2, 4096], P('section', 'chan'), may hold values from -4 to 4
- decay_param: float32 [2, 4096], P('section', 'chan')
- norm_gain: float32 [2, 4096], P('section', 'chan'), may hold values from 0.1 to 1.9
- doc_starts: int32 [4, 3], replicated, may hold values from 1 to 255
Outputs:
- input_grads: bfloat16 [2, 4, 256, 4096], P('section', None, 'seq', 'chan')
- rate_weight_grad: float32 [2, 16, 256, 256], P('section', 'chan')
- input_weight_grad: float32 [2, 16, 256, 256], P('section', 'chan')
- vector_grads: float32 [2, 3, 4096], P('section', None, 'chan')
The draws below stay inside these ranges and needn't reach their ends.
All inputs are finite; a program needn't handle non-finite values.
Results may differ from the reference program's by a relative error of at most 0.0055.
Values may be sent and summed in bfloat16 or wider, within the bound.
No kernel may reach another device: no remote copies, remote signals or barrier semaphores. Data moves between devices by JAX's collectives and lax.ppermute only.
A program may use at most 64 MiB of HBM per device.

```python
import math
import jax
import jax.numpy as jnp
from jax import lax

D = 4096
HEADS = 16
HEAD = 256
MICRO = 4
DOCS = 3
LAYERS = 2
SEQ_LEN = 256


def draw_layer_inputs(key, part):
    key_base = jax.random.fold_in(key, 0)
    key_column = jax.random.fold_in(key, 1)
    key_row = jax.random.fold_in(key, 2)
    key_sign = jax.random.fold_in(key, 4)
    key_level = jax.random.fold_in(key, 5)
    full_shape = (LAYERS, MICRO, SEQ_LEN, D)
    column_pos = jnp.arange(D, dtype=jnp.float32) / D
    column_scale = jnp.exp(column_pos * math.log(3.0) + jax.random.uniform(key_column, (D,), jnp.float32, 0.0, math.log(3.3)))
    row_scale = jnp.exp(jax.random.uniform(key_row, (LAYERS, MICRO, SEQ_LEN, 1), jnp.float32, 0.0, math.log(4.0)))
    offset_sign = jnp.where(jax.random.uniform(key_sign, (LAYERS, MICRO, 1, D), jnp.float32) < 0.5, -1.0, 1.0)
    offset_level = jax.random.uniform(key_level, (LAYERS, MICRO, 1, D), jnp.float32, 0.3, 0.7)
    channel_offset = offset_sign * offset_level
    base_draw = jax.random.normal(key_base, full_shape, jnp.float32)
    return ((base_draw + channel_offset) * row_scale * column_scale).astype(jnp.bfloat16)


def draw_out_grad(key, part):
    key_base = jax.random.fold_in(key, 0)
    key_column = jax.random.fold_in(key, 1)
    key_sign = jax.random.fold_in(key, 3)
    key_level = jax.random.fold_in(key, 4)
    full_shape = (MICRO, SEQ_LEN, D)
    ramp_scale = jnp.exp(jnp.arange(SEQ_LEN, dtype=jnp.float32) / SEQ_LEN * math.log(3.0))[None, :, None]
    column_scale = jnp.exp(jax.random.uniform(key_column, (D,), jnp.float32, 0.0, math.log(3.0)))
    offset_sign = jnp.where(jax.random.uniform(key_sign, (MICRO, 1, D), jnp.float32) < 0.5, -1.0, 1.0)
    offset_level = jax.random.uniform(key_level, (MICRO, 1, D), jnp.float32, 0.03, 0.07)
    channel_offset = offset_sign * offset_level
    base_draw = jax.random.normal(key_base, full_shape, jnp.float32)
    return ((base_draw + channel_offset) * ramp_scale * column_scale).astype(jnp.bfloat16)


def draw_decay_param(key, part):
    key_mask, key_fast, key_slow = jax.random.split(key, 3)
    fast_share = 0.5
    fast_mask = jax.random.uniform(key_mask, (LAYERS, D), jnp.float32) < fast_share
    rate_fast = jnp.exp(jax.random.uniform(key_fast, (LAYERS, D), jnp.float32, math.log(0.004), math.log(0.02)))
    rate_slow = jnp.exp(jax.random.uniform(key_slow, (LAYERS, D), jnp.float32, math.log(0.02 / SEQ_LEN), math.log(0.25 / SEQ_LEN)))
    rate_value = jnp.where(fast_mask, rate_fast, rate_slow)
    return -jnp.log(jnp.expm1(rate_value))


def touch_ends(values, rng, low, top_value):
    shape = values.shape
    index_at = [jax.random.randint(jax.random.fold_in(rng, axis), (), 0, shape[axis]) for axis in range(len(shape))]
    values = values.at[tuple(index_at)].set(low)
    longest = shape.index(max(shape))
    index_at[longest] = (index_at[longest] + 1) % shape[longest]
    return values.at[tuple(index_at)].set(top_value)


def level_of(rng, shape, pieces, smallest, top_value):
    loudness = 1.0
    for dim, shards_of in pieces:
        heights = jax.random.uniform(jax.random.fold_in(jax.random.fold_in(rng, 6), dim), (shards_of,), jnp.float32, smallest / len(pieces), top_value / len(pieces))
        loudness = loudness * jnp.repeat(jnp.exp(heights), shape[dim] // shards_of).reshape((-1,) + (1,) * (len(shape) - 1 - dim))
    return loudness


def bell_draw(own_key, dims, spread, most, cuts=(), kind=jnp.bfloat16):
    entries = spread * jax.random.normal(own_key, dims, jnp.float32)
    if cuts:
        entries = entries * level_of(own_key, dims, cuts, -0.22, 0.18)
    return jnp.clip(entries, -most, most).astype(kind)


def setup_inputs(seed: int = 0) -> dict:
    key_of = jax.random.split(jax.random.key(seed), 10)
    return {
        "layer_inputs": draw_layer_inputs(jax.random.fold_in(key_of[9], 71), 0),
        "out_grad": draw_out_grad(jax.random.fold_in(key_of[9], 71), 0),
        "rate_weight": bell_draw(key_of[2], (LAYERS, HEADS, HEAD, HEAD), HEAD ** -0.5, 0.375, ((0, 2), (1, 4))),
        "input_weight": bell_draw(key_of[3], (LAYERS, HEADS, HEAD, HEAD), HEAD ** -0.5, 0.375, ((0, 2), (1, 4))),
        "rate_bias": bell_draw(key_of[4], (LAYERS, D), 1.0, 4.0, ((0, 2), (1, 4)), jnp.float32),
        "input_bias": bell_draw(key_of[5], (LAYERS, D), 1.0, 4.0, ((0, 2), (1, 4)), jnp.float32),
        "decay_param": draw_decay_param(jax.random.fold_in(key_of[9], 71), 0),
        "norm_gain": jnp.clip(1.0 + 0.18 * jax.random.normal(key_of[7], (LAYERS, D), jnp.float32), 0.1, 1.9),
        "doc_starts": touch_ends(jax.random.randint(key_of[8], (MICRO, DOCS), 1, SEQ_LEN), jax.random.fold_in(key_of[8], 1), 1, SEQ_LEN - 1).astype(jnp.int32),
    }


def pair_combine(first_pair, second_pair):
    return (first_pair[0] * second_pair[0], second_pair[0] * first_pair[1] + second_pair[1])

def layer_backward(inputs, upstream, weights_both, bias_both, decay_row, gain_row, starts):
    seq_rows = inputs.shape[0]
    xfloat = inputs.astype(jnp.float32)
    inv_rms = lax.rsqrt(lax.optimization_barrier(jnp.sum(xfloat * xfloat, axis=1, keepdims=True)) / D + 1e-06)
    normed = (xfloat * inv_rms * gain_row).astype(jnp.bfloat16)
    normed_wide = normed.astype(jnp.float32)
    by_head = normed_wide.reshape(seq_rows, HEADS, HEAD)
    pre_both = jnp.einsum('shb,hbc->shc', by_head, weights_both.astype(jnp.float32))
    pre_rate = pre_both[:, :, :HEAD].reshape(seq_rows, D) + bias_both[0]
    pre_input = pre_both[:, :, HEAD:].reshape(seq_rows, D) + bias_both[1]
    rate_gate = jax.nn.sigmoid(pre_rate)
    input_gate = jax.nn.sigmoid(pre_input)
    soft_rate = jax.nn.softplus(-decay_row)
    log_decay = -8.0 * rate_gate * soft_rate
    position = jnp.arange(seq_rows, dtype=jnp.int32)
    is_reset = jnp.logical_or(position == 0, jnp.any(position[:, None] == starts[None, :], axis=1))[:, None]
    decay_eff = jnp.where(is_reset, 0.0, jnp.exp(log_decay))
    square_gap = jnp.exp(2.0 * log_decay)
    base_mult = jnp.sqrt(jnp.maximum(-jnp.expm1(2.0 * log_decay), 1e-06))
    multiplier = jnp.where(is_reset, 1.0, base_mult)
    lru_drive = multiplier * input_gate * normed_wide
    decay_prod, states = lax.associative_scan(pair_combine, (decay_eff, lru_drive), axis=0)
    prev_state = jnp.concatenate([jnp.zeros((1, D), jnp.float32), states[:-1]], axis=0)
    upstream_wide = upstream.astype(jnp.float32)
    next_decay = jnp.concatenate([decay_eff[1:], jnp.ones((1, D), jnp.float32)], axis=0)
    flip_pair = lax.associative_scan(pair_combine, (next_decay[::-1], upstream_wide[::-1]), axis=0)
    state_grad = flip_pair[1][::-1]
    grad_mult = state_grad * input_gate * normed_wide
    grad_log = state_grad * prev_state * decay_eff - jnp.where(is_reset, 0.0, grad_mult * square_gap / base_mult)
    grad_rate = (grad_log * (-8.0 * soft_rate) * rate_gate * (1.0 - rate_gate)).astype(jnp.bfloat16)
    grad_input = (state_grad * multiplier * normed_wide * input_gate * (1.0 - input_gate)).astype(jnp.bfloat16)
    grad_both = jnp.concatenate([grad_rate.reshape(seq_rows, HEADS, HEAD), grad_input.reshape(seq_rows, HEADS, HEAD)], axis=2).astype(jnp.float32)
    back_proj = jnp.einsum('shc,hbc->shb', grad_both, weights_both.astype(jnp.float32)).reshape(seq_rows, D)
    grad_normed = state_grad * multiplier * input_gate + back_proj
    scaled = grad_normed * gain_row
    cross_sum = lax.optimization_barrier(jnp.sum(xfloat * scaled, axis=1, keepdims=True)) / D
    input_grad = (upstream_wide + inv_rms * scaled - xfloat * inv_rms ** 3 * cross_sum).astype(jnp.bfloat16)
    weight_term = jnp.einsum('shb,shc->hbc', by_head, grad_both)
    vector_term = jnp.stack([lax.optimization_barrier(jnp.sum(grad_rate.astype(jnp.float32), axis=0)), lax.optimization_barrier(jnp.sum(grad_input.astype(jnp.float32), axis=0)), lax.optimization_barrier(jnp.sum(grad_normed * xfloat * inv_rms, axis=0))])
    return (input_grad, weight_term, vector_term)

def reference(layer_inputs, out_grad, rate_weight, input_weight, rate_bias, input_bias, decay_param, norm_gain, doc_starts):
    grad_scale = 1.0 / math.sqrt(MICRO * SEQ_LEN)
    upstream_list = [out_grad[micro_index] for micro_index in range(MICRO)]
    layer_grads = [None] * LAYERS
    layer_weights = [None] * LAYERS
    layer_vectors = [None] * LAYERS
    for layer_index in range(LAYERS - 1, -1, -1):
        weights_both = jnp.concatenate([rate_weight[layer_index], input_weight[layer_index]], axis=2)
        bias_both = jnp.stack([rate_bias[layer_index], input_bias[layer_index]])
        weight_total = jnp.zeros((HEADS, HEAD, 2 * HEAD), jnp.float32)
        vector_total = jnp.zeros((3, D), jnp.float32)
        results = []
        for micro_index in range(MICRO):
            input_grad, weight_term, vector_term = layer_backward(layer_inputs[layer_index, micro_index], upstream_list[micro_index], weights_both, bias_both, decay_param[layer_index], norm_gain[layer_index], doc_starts[micro_index])
            results.append(input_grad)
            weight_total = weight_total + weight_term
            vector_total = vector_total + vector_term
        upstream_list = results
        layer_grads[layer_index] = jnp.stack(results)
        layer_weights[layer_index] = weight_total * grad_scale
        layer_vectors[layer_index] = vector_total * grad_scale
    weight_stack = jnp.stack(layer_weights)
    return (jnp.stack(layer_grads), weight_stack[:, :, :, :HEAD], weight_stack[:, :, :, HEAD:], jnp.stack(layer_vectors))
```

```python
import functools
import math

import jax
import jax.numpy as jnp
from jax import lax
from jax.experimental import pallas as pl
from jax.experimental.pallas import tpu as pltpu
from jax.sharding import PartitionSpec as P

F32 = jnp.float32
BF16 = jnp.bfloat16
HIGH = lax.Precision.HIGHEST
VECTOR_ROWS = 16
DIRECT_RANKS = 4


def params(limit=24):
    return pltpu.CompilerParams(vmem_limit_bytes=limit * 1024 * 1024)


def cost(flops, size):
    return pl.CostEstimate(flops=flops, bytes_accessed=size, transcendentals=0)


def contract(a, b, dims, precision=None):
    return lax.dot_general(
        a, b, ((dims[:1], dims[1:]), ((), ())), precision=precision, preferred_element_type=F32
    )


def row_order(rows, tok_rows):
    shift = tok_rows.bit_length() - 1
    at = lax.broadcasted_iota(jnp.int32, (rows, rows), 0)
    source = lax.broadcasted_iota(jnp.int32, (rows, rows), 1)
    inner = jnp.bitwise_and(at, tok_rows - 1)
    wanted = (
        jnp.left_shift(jnp.right_shift(at, shift), shift)
        + jnp.bitwise_and(inner, 7) * (tok_rows // 8)
        + jnp.right_shift(inner, 3)
    )
    return jnp.where(wanted == source, 1.0, 0.0).astype(F32)


def to_column(parts):
    total = parts[0]
    for part in parts[1:]:
        total = total + part
    return contract(total, jnp.full((8, 128), 0.125, F32), (0, 0), HIGH)


def to_row(folded):
    return contract(jnp.ones((8, folded.shape[1]), F32), folded, (1, 1), HIGH)


def fold_lanes(value):
    total = value[:, :128]
    for at in range(128, value.shape[1], 128):
        total = total + value[:, at : at + 128]
    return total


def widen(column, width):
    return jnp.concatenate([column] * (width // 128), axis=1)


def square_kernel(x_ref, out_ref):
    total = None
    for at in range(0, x_ref.shape[1], 128):
        part = x_ref[:, at : at + 128].astype(F32)
        total = part * part if total is None else total + part * part
    out_ref[...] = to_row(total)


def permute_kernel(tok_rows, x_ref, up_ref, xp_ref, upp_ref):
    order = row_order(x_ref.shape[0], tok_rows).astype(BF16)
    width = 256
    for at in range(0, x_ref.shape[1], width):
        cols = slice(at, at + width)
        xp_ref[:, cols] = contract(order, x_ref[:, cols], (1, 0)).astype(BF16)
        upp_ref[:, cols] = contract(order, up_ref[:, cols], (1, 0)).astype(BF16)


def sublane_scan(decay, value, reverse):
    at = lax.broadcasted_iota(jnp.int32, decay.shape, 0)
    for step in (1, 2, 4):
        shift = 8 - step if reverse else step
        inside = at < 8 - step if reverse else at >= step
        value_far = pltpu.roll(value, shift, 0)
        decay_far = pltpu.roll(decay, shift, 0)
        value = jnp.where(inside, value + decay * value_far, value)
        decay = jnp.where(inside, decay * decay_far, decay)
    return decay, value


def reverse_blocks(decay_ref, up_ref, base, tok_rows, width):
    carry = jnp.zeros((8, width), F32)
    for pair in reversed(range(tok_rows // 16)):
        rows = pl.ds(base + 16 * pair, 16)
        decay = decay_ref[rows, :]
        upstream = up_ref[rows, :].astype(F32)
        carry = decay[8:] * (upstream[8:] + carry)
        carry = decay[:8] * (upstream[:8] + carry)
    return carry


def forward_kernel(
    micro_count,
    tok_rows,
    full_width,
    square_count,
    seq_at,
    starts,
    *refs,
):
    squares = refs[:square_count]
    (
        x_ref, up_ref, rw_ref, iw_ref, rb_ref, ib_ref, soft_ref, gain_ref,
        normed_ref, decay_ref, p1_ref, p2_ref, p3_ref, p4_ref,
        fdecay_ref, fstate_ref, rdecay_ref, rgrad_ref, pay_ref, inv_ref,
        keep_ref, prer_ref, prei_ref,
    ) = refs[square_count:]
    rows_total, width = x_ref.shape
    shift = tok_rows.bit_length() - 1

    @pl.when(pl.program_id(0) == 0)
    def _():
        column = to_column([part[...] for part in squares])
        order = row_order(rows_total, tok_rows)
        column = contract(order, column, (1, 0), HIGH)
        inv_ref[...] = lax.rsqrt(column / full_width + 1e-06)
        at = lax.broadcasted_iota(jnp.int32, (rows_total, 128), 0)
        inner = jnp.bitwise_and(at, tok_rows - 1)
        micro = jnp.right_shift(at, shift)
        position = (
            seq_at[0] * tok_rows
            + jnp.bitwise_and(inner, 7) * (tok_rows // 8)
            + jnp.right_shift(inner, 3)
        )
        reset = position == 0
        for m in range(micro_count):
            for d in range(starts.shape[1]):
                hit = jnp.logical_and(micro == m, position == starts[m, d])
                reset = jnp.logical_or(reset, hit)
        keep_ref[...] = jnp.where(reset, 0.0, 1.0)

    gain = gain_ref[...]
    normed = (x_ref[...].astype(F32) * widen(inv_ref[...], width) * gain).astype(BF16)
    normed_ref[...] = normed
    prer_ref[...] = contract(normed, rw_ref[0], (1, 0)) + rb_ref[...]
    prei_ref[...] = contract(normed, iw_ref[0], (1, 0)) + ib_ref[...]
    rate_scale = -8.0 * soft_ref[...]

    def per_micro(m, _):
        base = pl.multiple_of(m * tok_rows, tok_rows)
        state = jnp.zeros((8, width), F32)
        product = jnp.ones((8, width), F32)
        for pair in range(tok_rows // 16):
            rows = pl.ds(base + 16 * pair, 16)
            x_norm = normed_ref[rows, :].astype(F32)
            keep = widen(keep_ref[rows, :], width)
            rate_gate = 1.0 / (1.0 + jnp.exp(-prer_ref[rows, :]))
            input_gate = 1.0 / (1.0 + jnp.exp(-prei_ref[rows, :]))
            log_decay = rate_gate * rate_scale
            decay = jnp.exp(log_decay)
            square_gap = decay * decay
            twice = 2.0 * log_decay
            small = -twice * (
                1.0 + twice * (1 / 2 + twice * (1 / 6 + twice * (1 / 24 + twice * (1 / 120))))
            )
            gap = jnp.where(twice > -0.1, small, 1.0 - square_gap)
            gap = jnp.maximum(gap, 1e-06)
            inv_mult = lax.rsqrt(gap)
            multiplier = jnp.where(keep > 0.0, gap * inv_mult, 1.0)
            decay_eff = decay * keep
            rate_slope = rate_scale * rate_gate * (1.0 - rate_gate)
            gated = input_gate * x_norm
            passed = multiplier * input_gate
            drive = passed * x_norm
            decay_ref[rows, :] = decay_eff
            p1_ref[rows, :] = decay_eff * rate_slope
            p2_ref[rows, :] = keep * gated * square_gap * inv_mult * rate_slope
            p3_ref[rows, :] = drive * (1.0 - input_gate)
            p4_ref[rows, :] = passed
            for half in (slice(0, 8), slice(8, 16)):
                state = decay_eff[half] * state + drive[half]
                product = decay_eff[half] * product
        leaving = reverse_blocks(decay_ref, up_ref, base, tok_rows, width)
        fdecay, fstate = sublane_scan(product, state, False)
        rdecay, rgrad = sublane_scan(product, leaving, True)
        block_rows = pl.ds(pl.multiple_of(m * 8, 8), 8)
        fdecay_ref[block_rows, :] = fdecay
        fstate_ref[block_rows, :] = fstate
        rdecay_ref[block_rows, :] = rdecay
        rgrad_ref[block_rows, :] = rgrad
        pay_ref[pl.ds(m, 1), :] = fdecay[7:8]
        pay_ref[pl.ds(micro_count + m, 1), :] = fstate[7:8]
        pay_ref[pl.ds(2 * micro_count + m, 1), :] = rgrad[0:1]
        return 0

    lax.fori_loop(0, micro_count, per_micro, 0)


def leaving_kernel(micro_count, tok_rows, up_ref, decay_ref, rdecay_in, rgrad_ref, pay_ref):
    width = up_ref.shape[1]

    def per_micro(m, _):
        base = pl.multiple_of(m * tok_rows, tok_rows)
        carry = jnp.zeros((8, width), F32)
        product = jnp.ones((8, width), F32)
        for pair in reversed(range(tok_rows // 16)):
            rows = pl.ds(base + 16 * pair, 16)
            decay = decay_ref[rows, :]
            upstream = up_ref[rows, :].astype(F32)
            carry = decay[8:] * (upstream[8:] + carry)
            carry = decay[:8] * (upstream[:8] + carry)
            product = product * decay[8:] * decay[:8]
        _, rgrad = sublane_scan(product, carry, True)
        rgrad_ref[pl.ds(pl.multiple_of(m * 8, 8), 8), :] = rgrad
        pay_ref[pl.ds(m, 1), :] = rgrad[0:1]
        return 0

    lax.fori_loop(0, micro_count, per_micro, 0)


def ranked(refs, rank, at):
    if len(refs) == 1:
        return refs[0][at]
    chosen = refs[0][...]
    for k in range(1, len(refs)):
        chosen = jnp.where(jnp.bitwise_xor(rank, at) == k, refs[k][...], chosen)
    return chosen


def backward_kernel(
    micro_count,
    tok_rows,
    seq_count,
    pay_count,
    late_count,
    seq_at,
    *refs,
):
    pays = refs[:pay_count]
    lates = refs[pay_count : pay_count + late_count]
    (
        x_ref, up_ref, normed_ref, decay_ref, p1_ref, p2_ref, p3_ref, p4_ref,
        fdecay_ref, fstate_ref, rdecay_ref, rgrad_ref, inv_ref, gain_ref, rw_ref, iw_ref,
        part_ref, cross_ref, wr_ref, wi_ref,
        enter_ref, leave_ref, slope_ref, direct_ref, gr_ref, gi_ref, fold_ref,
    ) = refs[pay_count + late_count :]
    rows_total, width = x_ref.shape
    rank = seq_at[0]
    micro = micro_count

    state_in = jnp.zeros((micro, width), F32)
    grad_in = jnp.zeros((micro, width), F32)
    for at in range(seq_count):
        pay = ranked(pays, rank, at)
        state_in = jnp.where(
            at < rank, pay[micro : 2 * micro] + pay[:micro] * state_in, state_in
        )
    for at in reversed(range(seq_count)):
        pay = ranked(pays, rank, at)
        first = ranked(lates, rank, at) if late_count else pay[2 * micro :]
        grad_in = jnp.where(at > rank, first + pay[:micro] * grad_in, grad_in)
    enter_ref[...] = state_in
    leave_ref[...] = grad_in

    sub = lax.broadcasted_iota(jnp.int32, (8, width), 0)

    def per_micro(m, sums):
        sum_rate, sum_input = sums
        base = pl.multiple_of(m * tok_rows, tok_rows)
        block_rows = pl.ds(pl.multiple_of(m * 8, 8), 8)
        enter = enter_ref[pl.ds(m, 1), :]
        leave = leave_ref[pl.ds(m, 1), :]
        after = fstate_ref[block_rows, :] + fdecay_ref[block_rows, :] * enter
        state = jnp.where(sub == 0, enter, pltpu.roll(after, 1, 0))
        before = rgrad_ref[block_rows, :] + rdecay_ref[block_rows, :] * leave
        carry = jnp.where(sub == 7, leave, pltpu.roll(before, 7, 0))
        for pair in range(tok_rows // 16):
            rows = pl.ds(base + 16 * pair, 16)
            decay = decay_ref[rows, :]
            drive = p4_ref[rows, :] * normed_ref[rows, :].astype(F32)
            middle = decay[:8] * state + drive[:8]
            previous = jnp.concatenate([state, middle], axis=0)
            state = decay[8:] * middle + drive[8:]
            slope_ref[pl.ds(16 * pair, 16), :] = previous * p1_ref[rows, :] - p2_ref[rows, :]
        for pair in reversed(range(tok_rows // 16)):
            rows = pl.ds(base + 16 * pair, 16)
            decay = decay_ref[rows, :]
            upstream = up_ref[rows, :].astype(F32)
            late = upstream[8:] + carry
            early = upstream[:8] + decay[8:] * late
            carry = decay[:8] * early
            grad = jnp.concatenate([early, late], axis=0)
            grad_rate = (grad * slope_ref[pl.ds(16 * pair, 16), :]).astype(BF16)
            grad_input = (grad * p3_ref[rows, :]).astype(BF16)
            gr_ref[rows, :] = grad_rate
            gi_ref[rows, :] = grad_input
            direct_ref[rows, :] = grad * p4_ref[rows, :]
            wide_rate = grad_rate.astype(F32)
            wide_input = grad_input.astype(F32)
            sum_rate = sum_rate + wide_rate[:8] + wide_rate[8:]
            sum_input = sum_input + wide_input[:8] + wide_input[8:]
        return sum_rate, sum_input

    zero = jnp.zeros((8, width), F32)
    sum_rate, sum_input = lax.fori_loop(0, micro, per_micro, (zero, zero))

    normed = normed_ref[...]
    wr_ref[0, :width, :] = contract(normed, gr_ref[...], (0, 0)).astype(BF16)
    wi_ref[0, :width, :] = contract(normed, gi_ref[...], (0, 0)).astype(BF16)
    direct_ref[...] += contract(gr_ref[...], rw_ref[0], (1, 1)) + contract(
        gi_ref[...], iw_ref[0], (1, 1)
    )
    gain = gain_ref[...]

    def per_part(m, carry):
        sum_gain = carry
        rows = pl.ds(pl.multiple_of(m * tok_rows, tok_rows), tok_rows)
        inv = widen(inv_ref[rows, :], width)
        x = x_ref[rows, :].astype(F32)
        grad_normed = direct_ref[rows, :]
        scaled = grad_normed * gain
        part_ref[rows, :] = up_ref[rows, :].astype(F32) + inv * scaled
        weighted = grad_normed * x * inv
        folded = fold_lanes(x * scaled)

        @pl.when(pl.program_id(0) == 0)
        def _():
            fold_ref[rows, :] = folded

        @pl.when(pl.program_id(0) > 0)
        def _():
            fold_ref[rows, :] += folded

        for at in range(0, tok_rows, 8):
            sum_gain = sum_gain + weighted[at : at + 8]
        return sum_gain

    sum_gain = lax.fori_loop(0, micro, per_part, zero)
    vector = jnp.concatenate(
        [
            jnp.sum(sum_rate, axis=0, keepdims=True),
            jnp.sum(sum_input, axis=0, keepdims=True),
            jnp.sum(sum_gain, axis=0, keepdims=True),
            jnp.zeros((VECTOR_ROWS - 3, width), F32),
        ],
        axis=0,
    )
    high = vector.astype(BF16)
    wr_ref[0, width:, :] = high
    wi_ref[0, width:, :] = (vector - high.astype(F32)).astype(BF16)

    @pl.when(pl.program_id(0) == pl.num_programs(0) - 1)
    def _():
        cross_ref[...] = to_row(fold_ref[...])


def finish_block(part_ref, x_ref, inv, scale):
    return part_ref[...] - x_ref[...].astype(F32) * scale


def finish_kernel(full_width, cross_count, part_ref, x_ref, inv_ref, *refs):
    column = to_column([part[...] for part in refs[:cross_count]]) / full_width
    out_ref = refs[cross_count]
    inv = inv_ref[...]
    scale = inv * inv * inv * column
    for at in range(0, x_ref.shape[1], 128):
        cols = slice(at, at + 128)
        out_ref[:, cols] = (part_ref[:, cols] - x_ref[:, cols].astype(F32) * scale).astype(BF16)


def last_kernel(
    full_width, tok_rows, cross_count, section_at, part_ref, x_ref, inv_ref, early_ref, *refs
):
    column = to_column([part[...] for part in refs[:cross_count]]) / full_width
    out_ref = refs[cross_count]
    inv = inv_ref[...]
    scale = inv * inv * inv * column
    order = row_order(x_ref.shape[0], tok_rows).astype(BF16)
    bottom = section_at[0] == 0
    for at in range(0, x_ref.shape[1], 256):
        cols = slice(at, at + 256)
        value = part_ref[:, cols] - x_ref[:, cols].astype(F32) * widen(scale, 256)
        value = jnp.where(bottom, value.astype(BF16), early_ref[:, cols])
        out_ref[:, cols] = contract(order, value, (0, 0)).astype(BF16)


def owner_kernel(own_ref, *refs):
    total = own_ref[...].astype(F32)
    for part in refs[:-1]:
        total = total + part[...].astype(F32)
    refs[-1][...] = total.astype(BF16)


def exchange(value, axis):
    count = lax.axis_size(axis)
    if count != DIRECT_RANKS:
        return [lax.all_gather(value, axis)]
    return [value] + [
        lax.ppermute(value, axis, [(i, i ^ k) for i in range(count)]) for k in (3, 2, 1)[::-1]
    ]


def swap_sections(value):
    return lax.ppermute(value, "section", [(0, 1), (1, 0)])


def total_over_seq(value):
    count = lax.axis_size("seq")
    heads = value.shape[0]
    if count != DIRECT_RANKS or heads != count:
        return lax.psum(value.astype(F32), "seq").astype(BF16)
    rank = lax.axis_index("seq")
    taken = [
        lax.dynamic_index_in_dim(value, jnp.bitwise_xor(rank, k), 0, keepdims=False)
        for k in range(count)
    ]
    arrived = [
        lax.ppermute(taken[k], "seq", [(i, i ^ k) for i in range(count)]) for k in range(1, count)
    ]
    shape = value.shape[1:]
    owned = pl.pallas_call(
        owner_kernel, out_shape=jax.ShapeDtypeStruct(shape, BF16), compiler_params=params()
    )(taken[0], *arrived)
    back = [owned] + [
        lax.ppermute(owned, "seq", [(i, i ^ k) for i in range(count)]) for k in range(1, count)
    ]
    full = jnp.stack(back)
    return jnp.stack(
        [
            lax.dynamic_index_in_dim(full, jnp.bitwise_xor(rank, h), 0, keepdims=False)
            for h in range(count)
        ]
    )


def on_device(
    layer_inputs,
    out_grad,
    rate_weight,
    input_weight,
    rate_bias,
    input_bias,
    decay_param,
    norm_gain,
    doc_starts,
):
    micro, tok_rows, chan_width = out_grad.shape
    seq_count = lax.axis_size("seq")
    heads, size = rate_weight.shape[1:3]
    rows = micro * tok_rows
    full_width = chan_width * lax.axis_size("chan")
    grad_scale = 1.0 / math.sqrt(micro * tok_rows * seq_count)
    seq_at = lax.axis_index("seq").reshape(1).astype(jnp.int32)
    section = lax.axis_index("section")
    section_at = section.reshape(1).astype(jnp.int32)

    x_raw = layer_inputs.reshape(rows, chan_width)
    up_raw = out_grad.reshape(rows, chan_width)
    rate_weight, input_weight = rate_weight[0], input_weight[0]
    soft = jax.nn.softplus(-decay_param)

    def shape(dims, dtype=F32):
        return jax.ShapeDtypeStruct(dims, dtype)

    smem = pl.BlockSpec(memory_space=pltpu.SMEM)
    whole = pl.BlockSpec(memory_space=pltpu.VMEM)

    def col(lead):
        return pl.BlockSpec((lead, size), lambda h: (0, h))

    def fixed(dims):
        return pl.BlockSpec(dims, lambda h: (0,) * len(dims))

    head_block = pl.BlockSpec((1, size, size), lambda h: (h, 0, 0))

    squares = exchange(
        pl.pallas_call(
            square_kernel, out_shape=shape((8, rows)), compiler_params=params(),
            cost_estimate=cost(2 * rows * chan_width, 2 * rows * chan_width),
        )(x_raw),
        "chan",
    )
    if len(squares) == 1:
        squares = [squares[0][k] for k in range(lax.axis_size("chan"))]
    x, upstream = pl.pallas_call(
        functools.partial(permute_kernel, tok_rows),
        out_shape=(shape((rows, chan_width), BF16),) * 2,
        compiler_params=params(),
        cost_estimate=cost(4 * rows * rows * chan_width, 8 * rows * chan_width),
    )(x_raw, up_raw)

    row_vectors = [rate_bias, input_bias, soft, norm_gain]
    big = shape((rows, chan_width))
    blocks = shape((micro * 8, chan_width))
    forward = pl.pallas_call(
        functools.partial(forward_kernel, micro, tok_rows, full_width, len(squares)),
        grid=(heads,),
        in_specs=[smem, smem]
        + [fixed((8, rows))] * len(squares)
        + [col(rows)] * 2
        + [head_block] * 2
        + [col(1)] * 4,
        out_specs=[col(rows)] * 6 + [col(micro * 8)] * 4 + [col(3 * micro), fixed((rows, 128))],
        out_shape=[shape((rows, chan_width), BF16)]
        + [big] * 5
        + [blocks] * 4
        + [shape((3 * micro, chan_width)), shape((rows, 128))],
        scratch_shapes=[
            pltpu.VMEM((rows, 128), F32),
            pltpu.VMEM((rows, size), F32),
            pltpu.VMEM((rows, size), F32),
        ],
        compiler_params=params(),
        cost_estimate=cost(4 * rows * size * chan_width, 24 * rows * chan_width),
    )
    (
        normed, decay, p1, p2, p3, p4, fdecay, fstate, rdecay, rgrad, pay, inv,
    ) = forward(seq_at, doc_starts, *squares, x, upstream, rate_weight, input_weight, *row_vectors)
    pays = exchange(pay, "seq")

    def pay_spec(array):
        if array.ndim == 3:
            return pl.BlockSpec(array.shape[:2] + (size,), lambda h: (0, 0, h))
        return col(array.shape[0])

    def backward(upstream, rgrad, lates):
        wrows = size + VECTOR_ROWS
        wide = pl.BlockSpec((1, wrows, size), lambda h: (h, 0, 0))
        return pl.pallas_call(
            functools.partial(
                backward_kernel, micro, tok_rows, seq_count, len(pays), len(lates)
            ),
            grid=(heads,),
            in_specs=[smem]
            + [pay_spec(array) for array in pays + lates]
            + [col(rows)] * 8
            + [col(micro * 8)] * 4
            + [fixed((rows, 128)), col(1), head_block, head_block],
            out_specs=[col(rows), fixed((8, rows)), wide, wide],
            out_shape=[
                big,
                shape((8, rows)),
                shape((heads, wrows, size), BF16),
                shape((heads, wrows, size), BF16),
            ],
            scratch_shapes=[
                pltpu.VMEM((micro, size), F32),
                pltpu.VMEM((micro, size), F32),
                pltpu.VMEM((tok_rows, size), F32),
                pltpu.VMEM((rows, size), F32),
                pltpu.VMEM((rows, size), BF16),
                pltpu.VMEM((rows, size), BF16),
                pltpu.VMEM((rows, 128), F32),
            ],
            compiler_params=params(),
            cost_estimate=cost(8 * rows * size * chan_width, 30 * rows * chan_width),
        )(
            seq_at, *pays, *lates, x, upstream, normed, decay, p1, p2, p3, p4,
            fdecay, fstate, rdecay, rgrad, inv, norm_gain, rate_weight, input_weight,
        )

    def crossed(cross):
        parts = exchange(cross, "chan")
        if len(parts) == 1:
            parts = [parts[0][k] for k in range(lax.axis_size("chan"))]
        return parts

    part, cross, rate_top, input_top = backward(upstream, rgrad, [])
    cross_parts = crossed(cross)
    early = pl.pallas_call(
        functools.partial(finish_kernel, full_width, len(cross_parts)),
        in_specs=[whole] * (3 + len(cross_parts)),
        out_specs=whole,
        out_shape=shape((rows, chan_width), BF16),
        compiler_params=params(),
        cost_estimate=cost(4 * rows * chan_width, 8 * rows * chan_width),
    )(part, x, inv, *cross_parts)
    arrived = swap_sections(early)

    late_rgrad, late_pay = pl.pallas_call(
        functools.partial(leaving_kernel, micro, tok_rows),
        grid=(heads,),
        in_specs=[col(rows), col(rows), col(micro * 8)],
        out_specs=[col(micro * 8), col(micro)],
        out_shape=[blocks, shape((micro, chan_width))],
        compiler_params=params(),
        cost_estimate=cost(4 * rows * chan_width, 6 * rows * chan_width),
    )(arrived, decay, rdecay)
    lates = exchange(late_pay, "seq")
    part, cross, rate_low, input_low = backward(arrived, late_rgrad, lates)

    top = section == 1
    mine_top = jnp.where(top, input_top, swap_sections(rate_top))
    total_top = total_over_seq(mine_top)
    mine_low = jnp.where(top, swap_sections(input_low), rate_low)
    total_low = total_over_seq(mine_low)
    kept = jnp.where(top, total_top, total_low)
    other = swap_sections(jnp.where(top, total_low, total_top))
    rate_total = jnp.where(top, other, kept).astype(F32) * grad_scale
    input_total = jnp.where(top, kept, other).astype(F32) * grad_scale

    cross_parts = crossed(cross)
    grads = pl.pallas_call(
        functools.partial(last_kernel, full_width, tok_rows, len(cross_parts)),
        in_specs=[smem] + [whole] * (4 + len(cross_parts)),
        out_specs=whole,
        out_shape=shape((rows, chan_width), BF16),
        compiler_params=params(),
        cost_estimate=cost(2 * rows * rows * chan_width, 10 * rows * chan_width),
    )(section_at, part, x, inv, early, *cross_parts)

    vector = rate_total[:, size : size + 3] + input_total[:, size : size + 3]
    vector = jnp.swapaxes(vector, 0, 1).reshape(3, chan_width)
    return (
        grads.reshape(1, micro, tok_rows, chan_width),
        rate_total[None, :, :size],
        input_total[None, :, :size],
        vector[None],
    )


def solution(mesh):
    in_specs = (
        P("section", None, "seq", "chan"),
        P(None, "seq", "chan"),
        P("section", "chan", None, None),
        P("section", "chan", None, None),
        P("section", "chan"),
        P("section", "chan"),
        P("section", "chan"),
        P("section", "chan"),
        P(),
    )
    out_specs = (
        P("section", None, "seq", "chan"),
        P("section", "chan", None, None),
        P("section", "chan", None, None),
        P("section", None, "chan"),
    )
    return jax.shard_map(
        on_device, mesh=mesh, in_specs=in_specs, out_specs=out_specs, check_vma=False
    )
```

```python
import functools
import math

import jax
import jax.numpy as jnp
from jax import lax
from jax.experimental import pallas as pl
from jax.experimental.pallas import tpu as pltpu
from jax.sharding import PartitionSpec as P

F32 = jnp.float32
BF16 = jnp.bfloat16
HIGH = lax.Precision.HIGHEST
VECTOR_ROWS = 16
DIRECT_RANKS = 4


def params(limit=8):
    return pltpu.CompilerParams(vmem_limit_bytes=limit * 1024 * 1024)


def cost(flops, size):
    return pl.CostEstimate(flops=flops, bytes_accessed=size, transcendentals=0)


def contract(a, b, dims, precision=None):
    return lax.dot_general(
        a, b, ((dims[:1], dims[1:]), ((), ())), precision=precision, preferred_element_type=F32
    )


def row_order(rows, tok_rows):
    shift = tok_rows.bit_length() - 1
    at = lax.broadcasted_iota(jnp.int32, (rows, rows), 0)
    source = lax.broadcasted_iota(jnp.int32, (rows, rows), 1)
    inner = jnp.bitwise_and(at, tok_rows - 1)
    wanted = (
        jnp.left_shift(jnp.right_shift(at, shift), shift)
        + jnp.bitwise_and(inner, 7) * (tok_rows // 8)
        + jnp.right_shift(inner, 3)
    )
    return jnp.where(wanted == source, 1.0, 0.0).astype(F32)


def to_column(parts):
    total = parts[0]
    for part in parts[1:]:
        total = total + part
    return contract(total, jnp.full((8, 128), 0.125, F32), (0, 0), HIGH)


def to_row(folded):
    return contract(jnp.ones((8, folded.shape[1]), F32), folded, (1, 1), HIGH)


def fold_lanes(value):
    total = value[:, :128]
    for at in range(128, value.shape[1], 128):
        total = total + value[:, at : at + 128]
    return total


def widen(column, width):
    return jnp.concatenate([column] * (width // 128), axis=1)


def prepare_kernel(
    micro_count, tok_rows, section_at, seq_at, raw_starts, raw_x_ref, up_ref, rw_ref, iw_ref,
    rb_ref, ib_ref, dp_ref, gain_ref, square_ref, xk_ref, xs_ref, upp_ref, wk_ref, ws_ref,
    vk_ref, vs_ref, open_ref, starts, x_ref, raw_up_ref, raw_ref, sems,
):
    half = x_ref.shape[1] // 2
    heads = rw_ref.shape[0] // 2
    section = section_at[0]

    def columns(side):
        return pl.ds(pl.multiple_of(side * half, 128), half)

    moves = [(raw_x_ref, x_ref), (raw_starts, starts), (up_ref.at[:, columns(section)], raw_up_ref)]
    moves += [
        (source, raw_ref.at[k]) for k, source in enumerate((rb_ref, ib_ref, dp_ref, gain_ref))
    ]
    for side, w_out in ((section, wk_ref), (1 - section, ws_ref)):
        picked = pl.ds(side * heads, heads)
        moves += [
            (rw_ref.at[picked], w_out.at[pl.ds(0, heads)]),
            (iw_ref.at[picked], w_out.at[pl.ds(heads, heads)]),
        ]
    copies = [
        pltpu.make_async_copy(source, target, sems.at[k])
        for k, (source, target) in enumerate(moves)
    ]
    for copy in copies:
        copy.start()
    order = row_order(x_ref.shape[0], tok_rows).astype(BF16)
    copies[0].wait()
    total = None
    for side, x_out in ((section, xk_ref), (1 - section, xs_ref)):
        x = contract(order, x_ref[:, columns(side)], (1, 0))
        x_out[...] = x.astype(BF16)
        part = fold_lanes(x * x)
        total = part if total is None else total + part
    square_ref[...] = to_row(total)
    for copy in copies[1:]:
        copy.wait()
    upp_ref[...] = contract(order, raw_up_ref[...], (1, 0)).astype(BF16)
    for side, v_out in ((section, vk_ref), (1 - section, vs_ref)):
        rate_bias, input_bias, decay_param, gain = (
            raw_ref[k, :, columns(side)] for k in range(4)
        )
        slow = -decay_param
        soft = jnp.maximum(slow, 0.0) + jnp.log1p(jnp.exp(-jnp.abs(slow)))
        v_out[...] = jnp.concatenate(
            [rate_bias, input_bias, -8.0 * soft, gain, jnp.zeros((4, half), F32)], axis=0
        )
    shift = tok_rows.bit_length() - 1
    at = lax.broadcasted_iota(jnp.int32, open_ref.shape, 0)
    inner = jnp.bitwise_and(at, tok_rows - 1)
    micro = jnp.right_shift(at, shift)
    position = (
        seq_at[0] * tok_rows
        + jnp.bitwise_and(inner, 7) * (tok_rows // 8)
        + jnp.right_shift(inner, 3)
    )
    reset = position == 0
    for m in range(micro_count):
        for d in range(starts.shape[1]):
            hit = jnp.logical_and(micro == m, position == starts[m : m + 1, d : d + 1])
            reset = jnp.logical_or(reset, hit)
    open_ref[...] = jnp.where(reset, 0.0, 1.0)


def sublane_scan(decay, value, reverse):
    at = lax.broadcasted_iota(jnp.int32, decay.shape, 0)
    for step in (1, 2, 4):
        shift = 8 - step if reverse else step
        inside = at < 8 - step if reverse else at >= step
        value_far = pltpu.roll(value, shift, 0)
        decay_far = pltpu.roll(decay, shift, 0)
        value = jnp.where(inside, value + decay * value_far, value)
        decay = jnp.where(inside, decay * decay_far, decay)
    return decay, value


def reverse_blocks(decay_ref, up_ref, base, cols, tok_rows, width):
    carry = jnp.zeros((8, width), F32)
    for pair in reversed(range(tok_rows // 16)):
        rows = pl.ds(base + 16 * pair, 16)
        decay = decay_ref[rows, cols]
        upstream = up_ref[rows, cols].astype(F32)
        carry = decay[8:] * (upstream[8:] + carry)
        carry = decay[:8] * (upstream[:8] + carry)
    return carry


def send_rows(rank, ahead, behind, near_ref, far_ref):
    near_ref[...] = jnp.where(jnp.bitwise_and(rank, 1) == 0, ahead, behind)
    far_ref[...] = jnp.where(jnp.bitwise_and(rank, 2) == 0, ahead, behind)


def head_columns(head, width):
    return pl.ds(pl.multiple_of(head * width, width), width)


def forward_kernel(micro_count, tok_rows, full_width, layer, square_count, seq_at, section_at, *refs):
    own_squares, other_squares = refs[:square_count], refs[square_count]
    refs = refs[square_count + 1 :]
    open_ref, xk_ref, xr_ref, wk_ref, wr_ref, vk_ref, vr_ref = refs[:7]
    refs = refs[7:]
    if layer:
        up_ref, *refs = refs
    else:
        _above, *refs = refs
    normed_ref, factor_ref, block_ref, ahead_ref, inv_ref, *refs = refs
    decay_ref, p1_ref, p2_ref, p3_ref, p4_ref = (factor_ref.at[k] for k in range(5))
    fdecay_ref, fstate_ref, rdecay_ref = (block_ref.at[k] for k in range(3))
    if layer:
        rgrad_ref, behind_ref, near_ref, far_ref, *refs = refs
    prer_ref, prei_ref = refs
    width = wk_ref.shape[2]
    heads = xk_ref.shape[1] // width
    own = section_at[0] == layer

    total = jnp.where(own, sum(part[...] for part in own_squares), other_squares[...])
    inv_ref[...] = lax.rsqrt(to_column([total]) / full_width + 1e-06)

    def per_head(head, _):
        cols = head_columns(head, width)
        vectors = jnp.where(own, vk_ref[:, cols], vr_ref[:, cols])
        rate_scale, gain = vectors[2:3], vectors[3:4]
        x = jnp.where(own, xk_ref[:, cols], xr_ref[:, cols])
        normed = (x.astype(F32) * widen(inv_ref[...], width) * gain).astype(BF16)
        normed_ref[:, cols] = normed
        rate_weight = jnp.where(own, wk_ref[head], wr_ref[head])
        input_weight = jnp.where(own, wk_ref[heads + head], wr_ref[heads + head])
        prer_ref[...] = contract(normed, rate_weight, (1, 0)) + vectors[0:1]
        prei_ref[...] = contract(normed, input_weight, (1, 0)) + vectors[1:2]

        def per_micro(m, _):
            base = pl.multiple_of(m * tok_rows, tok_rows)
            state = jnp.zeros((8, width), F32)
            product = jnp.ones((8, width), F32)
            for pair in range(tok_rows // 16):
                rows = pl.ds(base + 16 * pair, 16)
                x_norm = normed_ref[rows, cols].astype(F32)
                keep = widen(open_ref[rows, :], width)
                rate_gate = 1.0 / (1.0 + jnp.exp(-prer_ref[rows, :]))
                input_gate = 1.0 / (1.0 + jnp.exp(-prei_ref[rows, :]))
                log_decay = rate_gate * rate_scale
                decay = jnp.exp(log_decay)
                square_gap = decay * decay
                twice = 2.0 * log_decay
                small = -twice * (
                    1.0 + twice * (1 / 2 + twice * (1 / 6 + twice * (1 / 24 + twice * (1 / 120))))
                )
                gap = jnp.where(twice > -0.1, small, 1.0 - square_gap)
                gap = jnp.maximum(gap, 1e-06)
                inv_mult = lax.rsqrt(gap)
                multiplier = jnp.where(keep > 0.0, gap * inv_mult, 1.0)
                decay_eff = decay * keep
                rate_slope = rate_scale * rate_gate * (1.0 - rate_gate)
                gated = input_gate * x_norm
                passed = multiplier * input_gate
                drive = passed * x_norm
                decay_ref[rows, cols] = decay_eff
                p1_ref[rows, cols] = decay_eff * rate_slope
                p2_ref[rows, cols] = keep * gated * square_gap * inv_mult * rate_slope
                p3_ref[rows, cols] = drive * (1.0 - input_gate)
                p4_ref[rows, cols] = passed
                for part in (slice(0, 8), slice(8, 16)):
                    state = decay_eff[part] * state + drive[part]
                    product = decay_eff[part] * product
            fdecay, fstate = sublane_scan(product, state, False)
            block_rows = pl.ds(pl.multiple_of(m * 8, 8), 8)
            fdecay_ref[block_rows, cols] = fdecay
            fstate_ref[block_rows, cols] = fstate
            ahead_ref[pl.ds(m, 1), cols] = fdecay[7:8]
            ahead_ref[pl.ds(micro_count + m, 1), cols] = fstate[7:8]
            if layer:
                leaving = reverse_blocks(decay_ref, up_ref, base, cols, tok_rows, width)
                rdecay, rgrad = sublane_scan(product, leaving, True)
                rgrad_ref[block_rows, cols] = rgrad
                behind_ref[pl.ds(m, 1), cols] = fdecay[7:8]
                behind_ref[pl.ds(micro_count + m, 1), cols] = rgrad[0:1]
            else:
                rdecay, _unused = sublane_scan(product, product, True)
            rdecay_ref[block_rows, cols] = rdecay
            return 0

        lax.fori_loop(0, micro_count, per_micro, 0)
        return 0

    lax.fori_loop(0, heads, per_head, 0)
    if layer:
        send_rows(seq_at[0], ahead_ref[...], behind_ref[...], near_ref, far_ref)


def late_kernel(
    micro_count, tok_rows, full_width, cross_count, seq_at, section_at, part_ref, xk_ref, xr_ref,
    inv_ref, factor_ref, ahead_ref, *refs
):
    crosses = refs[:cross_count]
    early_ref, rgrad_ref, behind_ref, near_ref, far_ref, scale_ref = refs[cross_count:]
    decay_ref = factor_ref.at[0]
    width = 256
    column = to_column([part[...] for part in crosses]) / full_width
    inv = inv_ref[...]
    scale_ref[...] = inv * inv * inv * column
    own = section_at[0] == 1

    def per_head(head, _):
        cols = head_columns(head, width)

        def per_micro(m, _):
            base = pl.multiple_of(m * tok_rows, tok_rows)
            carry = jnp.zeros((8, width), F32)
            product = jnp.ones((8, width), F32)
            for pair in reversed(range(tok_rows // 16)):
                rows = pl.ds(base + 16 * pair, 16)
                decay = decay_ref[rows, cols]
                x = jnp.where(own, xk_ref[rows, cols], xr_ref[rows, cols]).astype(F32)
                scale = widen(scale_ref[rows, :], width)
                early = (part_ref[rows, cols] - x * scale).astype(BF16)
                early_ref[rows, cols] = early
                upstream = early.astype(F32)
                carry = decay[8:] * (upstream[8:] + carry)
                carry = decay[:8] * (upstream[:8] + carry)
                product = product * decay[8:] * decay[:8]
            _, rgrad = sublane_scan(product, carry, True)
            rgrad_ref[pl.ds(pl.multiple_of(m * 8, 8), 8), cols] = rgrad
            behind_ref[pl.ds(m, 1), cols] = ahead_ref[pl.ds(m, 1), cols]
            behind_ref[pl.ds(micro_count + m, 1), cols] = rgrad[0:1]
            return 0

        lax.fori_loop(0, micro_count, per_micro, 0)
        return 0

    lax.fori_loop(0, part_ref.shape[1] // width, per_head, 0)
    send_rows(seq_at[0], ahead_ref[...], behind_ref[...], near_ref, far_ref)


def ranked(refs, rank, at):
    if len(refs) == 1:
        return refs[0][at]
    chosen = refs[0][...]
    for k in range(2, len(refs) + 1):
        chosen = jnp.where(jnp.bitwise_xor(rank, at) == k, refs[k - 1][...], chosen)
    return chosen


def backward_kernel(
    micro_count, tok_rows, seq_count, layer, direct, pay_count, seq_at, section_at, *refs
):
    pays = refs[:pay_count]
    (
        xk_ref, xr_ref, up_ref, normed_ref, factor_ref, block_ref, rgrad_ref, inv_ref,
        vk_ref, vr_ref, wk_ref, wr_ref, _before,
        part_ref, cross_ref, *unit_refs,
        enter_ref, leave_ref, slope_ref, direct_ref, gr_ref, gi_ref, fold_ref, weight_ref,
    ) = refs[pay_count:]
    decay_ref, p1_ref, p2_ref, p3_ref, p4_ref = (factor_ref.at[k] for k in range(5))
    fdecay_ref, fstate_ref, rdecay_ref = (block_ref.at[k] for k in range(3))
    width = wk_ref.shape[2]
    heads = xk_ref.shape[1] // width
    rank = seq_at[0]
    micro = micro_count
    own = section_at[0] == layer
    behind = 2 * micro if pay_count == 1 else 0

    state_in = jnp.zeros(enter_ref.shape, F32)
    grad_in = jnp.zeros(leave_ref.shape, F32)
    for at in range(seq_count - 1):
        pay = ranked(pays, rank, at)
        state_in = jnp.where(
            at < rank, pay[micro : 2 * micro] + pay[:micro] * state_in, state_in
        )
    for at in reversed(range(1, seq_count)):
        pay = ranked(pays, rank, at)[behind:]
        grad_in = jnp.where(
            at > rank, pay[micro : 2 * micro] + pay[:micro] * grad_in, grad_in
        )
    enter_ref[...] = state_in
    leave_ref[...] = grad_in
    fold_ref[...] = jnp.zeros(fold_ref.shape, F32)

    sub = lax.broadcasted_iota(jnp.int32, (8, width), 0)
    zero = jnp.zeros((8, width), F32)

    def per_head(head, _):
        cols = head_columns(head, width)

        def per_micro(m, sums):
            sum_rate, sum_input = sums
            base = pl.multiple_of(m * tok_rows, tok_rows)
            block_rows = pl.ds(pl.multiple_of(m * 8, 8), 8)
            enter = enter_ref[pl.ds(m, 1), cols]
            leave = leave_ref[pl.ds(m, 1), cols]
            after = fstate_ref[block_rows, cols] + fdecay_ref[block_rows, cols] * enter
            state = jnp.where(sub == 0, enter, pltpu.roll(after, 1, 0))
            before = rgrad_ref[block_rows, cols] + rdecay_ref[block_rows, cols] * leave
            carry = jnp.where(sub == 7, leave, pltpu.roll(before, 7, 0))
            for pair in range(tok_rows // 16):
                rows = pl.ds(base + 16 * pair, 16)
                decay = decay_ref[rows, cols]
                drive = p4_ref[rows, cols] * normed_ref[rows, cols].astype(F32)
                middle = decay[:8] * state + drive[:8]
                previous = jnp.concatenate([state, middle], axis=0)
                state = decay[8:] * middle + drive[8:]
                slope_ref[pl.ds(16 * pair, 16), :] = (
                    previous * p1_ref[rows, cols] - p2_ref[rows, cols]
                )
            for pair in reversed(range(tok_rows // 16)):
                rows = pl.ds(base + 16 * pair, 16)
                decay = decay_ref[rows, cols]
                upstream = up_ref[rows, cols].astype(F32)
                late = upstream[8:] + carry
                early = upstream[:8] + decay[8:] * late
                carry = decay[:8] * early
                grad = jnp.concatenate([early, late], axis=0)
                grad_rate = (grad * slope_ref[pl.ds(16 * pair, 16), :]).astype(BF16)
                grad_input = (grad * p3_ref[rows, cols]).astype(BF16)
                gr_ref[rows, :] = grad_rate
                gi_ref[rows, :] = grad_input
                direct_ref[rows, :] = grad * p4_ref[rows, cols]
                wide_rate = grad_rate.astype(F32)
                wide_input = grad_input.astype(F32)
                sum_rate = sum_rate + wide_rate[:8] + wide_rate[8:]
                sum_input = sum_input + wide_input[:8] + wide_input[8:]
            return sum_rate, sum_input

        sum_rate, sum_input = lax.fori_loop(0, micro, per_micro, (zero, zero))

        normed = normed_ref[:, cols]
        places = [jnp.bitwise_xor(2 * head + gate, rank if direct else 0) for gate in range(2)]
        for place, grad_ref in zip(places, (gr_ref, gi_ref)):
            unit_ref = weight_ref.at[place]
            unit_ref[:width, :] = contract(normed, grad_ref[...], (0, 0)).astype(BF16)
        rate_weight = jnp.where(own, wk_ref[head], wr_ref[head])
        input_weight = jnp.where(own, wk_ref[heads + head], wr_ref[heads + head])
        direct_ref[...] += contract(gr_ref[...], rate_weight, (1, 1)) + contract(
            gi_ref[...], input_weight, (1, 1)
        )
        gain = jnp.where(own, vk_ref[3:4, cols], vr_ref[3:4, cols])

        def per_part(m, sum_gain):
            rows = pl.ds(pl.multiple_of(m * tok_rows, tok_rows), tok_rows)
            inv = widen(inv_ref[rows, :], width)
            x = jnp.where(own, xk_ref[rows, cols], xr_ref[rows, cols]).astype(F32)
            grad_normed = direct_ref[rows, :]
            scaled = grad_normed * gain
            part_ref[rows, cols] = up_ref[rows, cols].astype(F32) + inv * scaled
            weighted = grad_normed * x * inv
            fold_ref[rows, :] += fold_lanes(x * scaled)
            for at in range(0, tok_rows, 8):
                sum_gain = sum_gain + weighted[at : at + 8]
            return sum_gain

        sum_gain = lax.fori_loop(0, micro, per_part, zero)
        vector = jnp.concatenate(
            [
                jnp.sum(sum_rate, axis=0, keepdims=True),
                jnp.sum(sum_input, axis=0, keepdims=True),
                jnp.sum(sum_gain, axis=0, keepdims=True),
                jnp.zeros((VECTOR_ROWS - 3, width), F32),
            ],
            axis=0,
        )
        high = vector.astype(BF16)
        weight_ref[places[0], width:, :] = high
        weight_ref[places[1], width:, :] = (vector - high.astype(F32)).astype(BF16)
        return 0

    lax.fori_loop(0, heads, per_head, 0)
    cross_ref[...] = to_row(fold_ref[...])
    if not direct:
        unit_refs[0][...] = weight_ref[...]
    elif layer:
        keep_ref, send_ref = unit_refs
        for k in range(4):
            (send_ref if k % 2 else keep_ref)[k // 2] = weight_ref[k]
    else:
        for k, unit_ref in enumerate(unit_refs):
            unit_ref[...] = weight_ref[k]


def last_kernel(
    full_width, tok_rows, cross_count, section_at, part_ref, xk_ref, xr_ref, inv_ref, early_ref,
    *refs
):
    column = to_column([part[...] for part in refs[:cross_count]]) / full_width
    keep_ref, send_ref = refs[cross_count:]
    inv = inv_ref[...]
    scale = inv * inv * inv * column
    order = row_order(xk_ref.shape[0], tok_rows).astype(BF16)
    bottom = section_at[0] == 0
    for at in range(0, xk_ref.shape[1], 256):
        cols = slice(at, at + 256)
        x = jnp.where(bottom, xk_ref[:, cols], xr_ref[:, cols]).astype(F32)
        value = (part_ref[:, cols] - x * widen(scale, 256)).astype(BF16)
        early = early_ref[:, cols]
        keep_ref[:, cols] = contract(order, jnp.where(bottom, value, early), (0, 0)).astype(BF16)
        send_ref[:, cols] = contract(order, jnp.where(bottom, early, value), (0, 0)).astype(BF16)


def join_kernel(section_at, keep_ref, arrived_ref, out_ref):
    half = keep_ref.shape[1]
    mine = section_at[0] * half
    out_ref[:, pl.ds(pl.multiple_of(mine, 128), half)] = keep_ref[...]
    out_ref[:, pl.ds(pl.multiple_of(half - mine, 128), half)] = arrived_ref[...]


def add_kernel(*refs):
    total = refs[0][...].astype(F32)
    for part in refs[1:-1]:
        total = total + part[...].astype(F32)
    refs[-1][...] = total.astype(refs[-1].dtype)


def add_pairs_kernel(a_ref, b_ref, *outs):
    for k, out_ref in enumerate(outs):
        out_ref[...] = (a_ref[k].astype(F32) + b_ref[k].astype(F32)).astype(out_ref.dtype)


def weights_kernel(units, scale, section_at, unit_at, *refs):
    tops, lows, others = refs[:units], refs[units : 2 * units], refs[2 * units : 3 * units]
    rate_ref, input_ref, vector_ref = refs[3 * units :]
    head = pl.program_id(0)
    size = rate_ref.shape[1]
    half_heads = units // 2
    section = section_at[0]
    mine = head // half_heads == section
    local = head % half_heads
    for gate, out_ref in enumerate((rate_ref, input_ref)):
        index = jnp.bitwise_xor(2 * local + gate, unit_at[0])
        for k in range(units):
            here = index == k
            sources = (
                (jnp.logical_and(mine, section == 1), tops[k]),
                (jnp.logical_and(mine, section == 0), lows[k]),
                (jnp.logical_not(mine), others[k]),
            )
            for wanted, source in sources:

                @pl.when(jnp.logical_and(here, wanted))
                def _(source=source, gate=gate, out_ref=out_ref):
                    out_ref[0] = source[:size, :].astype(F32) * scale
                    rows = source[size:, :].astype(F32) * scale
                    if gate == 0:
                        vector_ref[:, 0, :] = rows[:3]
                    else:
                        vector_ref[:, 0, :] += rows[:3]


def xor_moves(value, axis, k):
    return lax.ppermute(value, axis, [(i, i ^ k) for i in range(lax.axis_size(axis))])


def swap_sections(value):
    return lax.ppermute(value, "section", [(0, 1), (1, 0)])


def chan_parts(value):
    count = lax.axis_size("chan")
    if count & (count - 1):
        gathered = lax.all_gather(value, "chan")
        return [gathered[k] for k in range(count)]
    return [xor_moves(value, "chan", k) for k in reversed(range(1, count))] + [value]


def seq_pays(ahead, behind, near, far):
    if lax.axis_size("seq") != DIRECT_RANKS:
        return [lax.all_gather(jnp.concatenate([ahead, behind], axis=0), "seq")]
    return [xor_moves(far, "seq", 3), xor_moves(far, "seq", 2), xor_moves(near, "seq", 1)][::-1]


def add_units(value, *others):
    return pl.pallas_call(
        add_kernel,
        out_shape=jax.ShapeDtypeStruct(value.shape, value.dtype),
        compiler_params=params(),
        cost_estimate=cost(0, 8 * value.size),
    )(value, *others)


def add_pairs(a, b):
    return pl.pallas_call(
        add_pairs_kernel,
        out_shape=[jax.ShapeDtypeStruct(a.shape[1:], a.dtype)] * a.shape[0],
        compiler_params=params(),
        cost_estimate=cost(0, 6 * a.size),
    )(a, b)


def after(value, *others):
    return lax.optimization_barrier((value, *others))[0]


def on_device(
    layer_inputs,
    out_grad,
    rate_weight,
    input_weight,
    rate_bias,
    input_bias,
    decay_param,
    norm_gain,
    doc_starts,
):
    micro, tok_rows, chan_width = out_grad.shape
    seq_count = lax.axis_size("seq")
    heads, size = rate_weight.shape[1:3]
    half_heads = heads // 2
    half = chan_width // 2
    rows = micro * tok_rows
    full_width = chan_width * lax.axis_size("chan")
    grad_scale = 1.0 / math.sqrt(micro * tok_rows * seq_count)
    seq_at = lax.axis_index("seq").reshape(1).astype(jnp.int32)
    section = lax.axis_index("section")
    section_at = section.reshape(1).astype(jnp.int32)

    x_raw = layer_inputs.reshape(rows, chan_width)
    up_raw = out_grad.reshape(rows, chan_width)

    def shape(dims, dtype=F32):
        return jax.ShapeDtypeStruct(dims, dtype)

    smem = pl.BlockSpec(memory_space=pltpu.SMEM)
    whole = pl.BlockSpec(memory_space=pltpu.VMEM)

    def call(kernel, scalars, arrays, outs, scratch=(), flops=0, size_bytes=0, specs=None):
        return pl.pallas_call(
            kernel,
            in_specs=[smem] * len(scalars) + (specs or [whole] * len(arrays)),
            out_shape=outs,
            scratch_shapes=[
                pltpu.VMEM(*entry) if isinstance(entry, tuple) else entry for entry in scratch
            ],
            compiler_params=params(),
            cost_estimate=cost(flops, size_bytes),
        )(*scalars, *arrays)

    half_x = shape((rows, half), BF16)
    half_w = shape((heads, size, size), BF16)
    half_v = shape((8, half))
    square, x_keep, x_send, upstream, w_keep, w_send, v_keep, v_send, opened = call(
        functools.partial(prepare_kernel, micro, tok_rows),
        [section_at, seq_at],
        [
            pltpu.with_memory_space_constraint(array, pltpu.HBM)
            for array in (
                doc_starts, x_raw, up_raw, rate_weight[0], input_weight[0],
                rate_bias, input_bias, decay_param, norm_gain,
            )
        ],
        [shape((8, rows)), half_x, half_x, half_x, half_w, half_w, half_v, half_v, shape((rows, 128))],
        [
            (doc_starts.shape, jnp.int32),
            ((rows, chan_width), BF16),
            ((rows, half), BF16),
            ((4, 1, chan_width), F32),
            pltpu.SemaphoreType.DMA((11,)),
        ],
        specs=[pl.BlockSpec(memory_space=pltpu.HBM)] * 9,
        flops=4 * rows * rows * chan_width,
        size_bytes=12 * rows * chan_width,
    )
    own_squares = chan_parts(square)
    other_squares = swap_sections(add_units(*own_squares))
    x_got, w_got, v_got = (swap_sections(value) for value in (x_send, w_send, v_send))

    big = shape((rows, half))
    blocks = shape((micro * 8, half))
    pay = shape((2 * micro, half))

    def forward(layer, beside):
        return call(
            functools.partial(
                forward_kernel, micro, tok_rows, full_width, layer, len(own_squares)
            ),
            [seq_at, section_at],
            [
                *own_squares, other_squares, opened, x_keep, x_got, w_keep, w_got, v_keep, v_got,
                beside,
            ],
            [half_x, shape((5, rows, half)), shape((3, micro * 8, half)), pay, shape((rows, 128))]
            + ([blocks] + [pay] * 3) * layer,
            [((rows, size), F32)] * 2,
            flops=4 * rows * size * half,
            size_bytes=24 * rows * half,
        )

    direct = seq_count == DIRECT_RANKS and heads == DIRECT_RANKS
    unit_dims = {0: [()] * 4, 1: [(2,)] * 2} if direct else {0: [(heads,)], 1: [(heads,)]}

    def backward(layer, pays, upstream, kept, rgrad, before):
        normed, factors, block, _, inv = kept
        return call(
            functools.partial(
                backward_kernel, micro, tok_rows, seq_count, layer, direct, len(pays)
            ),
            [seq_at, section_at],
            [
                *pays, x_keep, x_got, upstream, normed, factors, block, rgrad, inv,
                v_keep, v_got, w_keep, w_got, before,
            ],
            [big, shape((8, rows))]
            + [shape(dims + (size + VECTOR_ROWS, size), BF16) for dims in unit_dims[layer]],
            [
                ((micro, half), F32),
                ((micro, half), F32),
                ((tok_rows, size), F32),
                ((rows, size), F32),
                ((rows, size), BF16),
                ((rows, size), BF16),
                ((rows, 128), F32),
                ((heads, size + VECTOR_ROWS, size), BF16),
            ],
            flops=8 * rows * size * half,
            size_bytes=30 * rows * half,
        )

    def chip_sum(value):
        return add_units(value, swap_sections(value))

    *top, top_rgrad, behind, near, far = forward(1, upstream)
    pays = seq_pays(top[3], behind, near, far)
    low = forward(0, top[1])
    part, cross, *top_parts = backward(1, pays, upstream, top, top_rgrad, low[3])
    parts = chan_parts(chip_sum(cross))
    if direct:
        arrived = xor_moves(top_parts[1], "seq", 1)
    early, low_rgrad, behind, near, far = call(
        functools.partial(late_kernel, micro, tok_rows, full_width, len(parts)),
        [seq_at, section_at],
        [part, x_keep, x_got, top[4], low[1], low[3], *parts],
        [half_x, blocks] + [pay] * 3,
        [((rows, 128), F32)],
        flops=8 * rows * half,
        size_bytes=12 * rows * half,
    )
    pays = seq_pays(low[3], behind, near, far)
    if direct:
        own_pair, far_pair = add_pairs(top_parts[0], after(arrived, near))
        arrived = xor_moves(far_pair, "seq", 2)
        top_own = add_units(own_pair, after(arrived, *pays))
        top_far = xor_moves(top_own, "seq", 2)
    part, cross, *low_parts = backward(
        0, pays, early, low, low_rgrad, top_own if direct else behind
    )
    parts = chan_parts(chip_sum(cross))
    if direct:
        place = lax.axis_index("seq")
        low_arrived = [xor_moves(low_parts[k], "seq", k) for k in (3, 2, 1)]
        low_arrived, parts = lax.optimization_barrier((low_arrived, parts))
        low_own = add_units(low_parts[0], *low_arrived)
        low_units = [low_own] + [xor_moves(low_own, "seq", k) for k in (1, 2, 3)]
        pair = xor_moves(jnp.stack([top_own, after(top_far, low_own)]), "seq", 1)
        top_units = [top_own, pair[0], top_far, pair[1]]
    else:
        place = jnp.zeros((), jnp.int32)
        top_units, low_units = (
            [total[k] for k in range(heads)]
            for total in (
                lax.psum(value.astype(F32), "seq").astype(BF16)
                for value in (top_parts[0], low_parts[0])
            )
        )
    grads_keep, grads_send = call(
        functools.partial(last_kernel, full_width, tok_rows, len(parts)),
        [section_at],
        [part, x_keep, x_got, low[4], early, *parts],
        [half_x, half_x],
        flops=4 * rows * rows * half,
        size_bytes=12 * rows * half,
    )
    grads = call(
        join_kernel, [section_at], [grads_keep, swap_sections(grads_send)],
        shape((rows, chan_width), BF16), size_bytes=4 * rows * chan_width,
    )
    if direct:
        grads, top_units, low_units = lax.optimization_barrier((grads, top_units, low_units))

    other_units = [
        swap_sections(jnp.where(section == 1, b, a)) for a, b in zip(top_units, low_units)
    ]
    out_block = pl.BlockSpec((1, size, size), lambda h: (h, 0, 0))
    rate_total, input_total, vector = pl.pallas_call(
        functools.partial(weights_kernel, heads, grad_scale),
        grid=(heads,),
        in_specs=[smem, smem] + [whole] * (3 * heads),
        out_specs=[out_block, out_block, pl.BlockSpec((3, 1, size), lambda h: (0, 0, h))],
        out_shape=[
            shape((heads, size, size)),
            shape((heads, size, size)),
            shape((3, 1, chan_width)),
        ],
        compiler_params=params(),
        cost_estimate=cost(0, 8 * heads * size * size),
    )(
        section_at, place.reshape(1).astype(jnp.int32), *top_units, *low_units, *other_units
    )
    return (
        grads.reshape(1, micro, tok_rows, chan_width),
        rate_total[None],
        input_total[None],
        jnp.swapaxes(vector, 0, 1),
    )


def solution(mesh):
    in_specs = (
        P("section", None, "seq", "chan"),
        P(None, "seq", "chan"),
        P("section", "chan", None, None),
        P("section", "chan", None, None),
        P("section", "chan"),
        P("section", "chan"),
        P("section", "chan"),
        P("section", "chan"),
        P(),
    )
    out_specs = (
        P("section", None, "seq", "chan"),
        P("section", "chan", None, None),
        P("section", "chan", None, None),
        P("section", None, "chan"),
    )
    return jax.shard_map(
        on_device, mesh=mesh, in_specs=in_specs, out_specs=out_specs, check_vma=False
    )
```

```python
import functools
import math

import jax
import jax.numpy as jnp
from jax import lax
from jax.experimental import pallas as pl
from jax.experimental.pallas import tpu as pltpu
from jax.sharding import PartitionSpec as P

F32 = jnp.float32
BF16 = jnp.bfloat16
HIGH = lax.Precision.HIGHEST
VECTOR_ROWS = 16
DIRECT_RANKS = 4


def params(limit=8):
    return pltpu.CompilerParams(vmem_limit_bytes=limit * 1024 * 1024)


def cost(flops, size):
    return pl.CostEstimate(flops=flops, bytes_accessed=size, transcendentals=0)


def contract(a, b, dims, precision=None):
    return lax.dot_general(
        a, b, ((dims[:1], dims[1:]), ((), ())), precision=precision, preferred_element_type=F32
    )


def row_order(rows, tok_rows):
    shift = tok_rows.bit_length() - 1
    at = lax.broadcasted_iota(jnp.int32, (rows, rows), 0)
    source = lax.broadcasted_iota(jnp.int32, (rows, rows), 1)
    inner = jnp.bitwise_and(at, tok_rows - 1)
    wanted = (
        jnp.left_shift(jnp.right_shift(at, shift), shift)
        + jnp.bitwise_and(inner, 7) * (tok_rows // 8)
        + jnp.right_shift(inner, 3)
    )
    return jnp.where(wanted == source, 1.0, 0.0).astype(F32)


def to_column(parts):
    total = parts[0]
    for part in parts[1:]:
        total = total + part
    return contract(total, jnp.full((8, 128), 0.125, F32), (0, 0), HIGH)


def to_row(folded):
    return contract(jnp.ones((8, folded.shape[1]), F32), folded, (1, 1), HIGH)


def fold_lanes(value):
    total = value[:, :128]
    for at in range(128, value.shape[1], 128):
        total = total + value[:, at : at + 128]
    return total


def widen(column, width):
    return jnp.concatenate([column] * (width // 128), axis=1)


def prepare_kernel(
    micro_count, tok_rows, section_at, seq_at, raw_starts, raw_x_ref, up_ref, rw_ref, iw_ref,
    rb_ref, ib_ref, dp_ref, gain_ref, square_ref, xk_ref, xs_ref, upp_ref, wk_ref, ws_ref,
    vk_ref, vs_ref, open_ref, starts, x_ref, raw_up_ref, raw_ref, sems,
):
    half = x_ref.shape[1] // 2
    heads = rw_ref.shape[0] // 2
    section = section_at[0]

    def columns(side):
        return pl.ds(pl.multiple_of(side * half, 128), half)

    moves = [(raw_x_ref, x_ref), (raw_starts, starts), (up_ref.at[:, columns(section)], raw_up_ref)]
    moves += [
        (source, raw_ref.at[k]) for k, source in enumerate((rb_ref, ib_ref, dp_ref, gain_ref))
    ]
    for side, w_out in ((section, wk_ref), (1 - section, ws_ref)):
        picked = pl.ds(side * heads, heads)
        moves += [
            (rw_ref.at[picked], w_out.at[pl.ds(0, heads)]),
            (iw_ref.at[picked], w_out.at[pl.ds(heads, heads)]),
        ]
    copies = [
        pltpu.make_async_copy(source, target, sems.at[k])
        for k, (source, target) in enumerate(moves)
    ]
    for copy in copies:
        copy.start()
    order = row_order(x_ref.shape[0], tok_rows).astype(BF16)
    copies[0].wait()
    total = None
    for side, x_out in ((section, xk_ref), (1 - section, xs_ref)):
        x = contract(order, x_ref[:, columns(side)], (1, 0))
        x_out[...] = x.astype(BF16)
        part = fold_lanes(x * x)
        total = part if total is None else total + part
    square_ref[...] = to_row(total)
    for copy in copies[1:]:
        copy.wait()
    upp_ref[...] = contract(order, raw_up_ref[...], (1, 0)).astype(BF16)
    for side, v_out in ((section, vk_ref), (1 - section, vs_ref)):
        rate_bias, input_bias, decay_param, gain = (
            raw_ref[k, :, columns(side)] for k in range(4)
        )
        slow = -decay_param
        soft = jnp.maximum(slow, 0.0) + jnp.log1p(jnp.exp(-jnp.abs(slow)))
        v_out[...] = jnp.concatenate(
            [rate_bias, input_bias, -8.0 * soft, gain, jnp.zeros((4, half), F32)], axis=0
        )
    shift = tok_rows.bit_length() - 1
    at = lax.broadcasted_iota(jnp.int32, open_ref.shape, 0)
    inner = jnp.bitwise_and(at, tok_rows - 1)
    micro = jnp.right_shift(at, shift)
    position = (
        seq_at[0] * tok_rows
        + jnp.bitwise_and(inner, 7) * (tok_rows // 8)
        + jnp.right_shift(inner, 3)
    )
    reset = position == 0
    for m in range(micro_count):
        for d in range(starts.shape[1]):
            hit = jnp.logical_and(micro == m, position == starts[m : m + 1, d : d + 1])
            reset = jnp.logical_or(reset, hit)
    open_ref[...] = jnp.where(reset, 0.0, 1.0)


def sublane_scan(decay, value, reverse):
    at = lax.broadcasted_iota(jnp.int32, decay.shape, 0)
    for step in (1, 2, 4):
        shift = 8 - step if reverse else step
        inside = at < 8 - step if reverse else at >= step
        value_far = pltpu.roll(value, shift, 0)
        decay_far = pltpu.roll(decay, shift, 0)
        value = jnp.where(inside, value + decay * value_far, value)
        decay = jnp.where(inside, decay * decay_far, decay)
    return decay, value


def reverse_blocks(decay_ref, up_ref, base, cols, tok_rows, width):
    carry = jnp.zeros((8, width), F32)
    for pair in reversed(range(tok_rows // 16)):
        rows = pl.ds(base + 16 * pair, 16)
        decay = decay_ref[rows, cols]
        upstream = up_ref[rows, cols].astype(F32)
        carry = decay[8:] * (upstream[8:] + carry)
        carry = decay[:8] * (upstream[:8] + carry)
    return carry


def pair_ends_kernel(micro, seq_at, own_ref, near_ref, out_ref):
    own, near = own_ref[...], near_ref[...]
    odd = jnp.bitwise_and(seq_at[0], 1) == 1
    first = jnp.where(odd, near, own)
    last = jnp.where(odd, own, near)
    state = last[micro : 2 * micro] + last[:micro] * first[micro : 2 * micro]
    grad = first[2 * micro :] + first[:micro] * last[2 * micro :]
    out_ref[...] = jnp.where(jnp.bitwise_and(seq_at[0], 2) == 0, state, grad)


def head_columns(head, width):
    return pl.ds(pl.multiple_of(head * width, width), width)


def forward_kernel(micro_count, tok_rows, full_width, layer, square_count, seq_at, section_at, *refs):
    own_squares, other_squares = refs[:square_count], refs[square_count]
    refs = refs[square_count + 1 :]
    open_ref, xk_ref, xr_ref, wk_ref, wr_ref, vk_ref, vr_ref = refs[:7]
    refs = refs[7:]
    if layer:
        up_ref, *refs = refs
    else:
        _above, *refs = refs
    normed_ref, factor_ref, block_ref, ahead_ref, inv_ref, *refs = refs
    decay_ref, p1_ref, p2_ref, p3_ref, p4_ref = (factor_ref.at[k] for k in range(5))
    fdecay_ref, fstate_ref, rdecay_ref = (block_ref.at[k] for k in range(3))
    if layer:
        rgrad_ref, *refs = refs
    prer_ref, prei_ref = refs
    width = wk_ref.shape[2]
    heads = xk_ref.shape[1] // width
    own = section_at[0] == layer

    total = jnp.where(own, sum(part[...] for part in own_squares), other_squares[...])
    inv_ref[...] = lax.rsqrt(to_column([total]) / full_width + 1e-06)

    def per_head(head, _):
        cols = head_columns(head, width)
        vectors = jnp.where(own, vk_ref[:, cols], vr_ref[:, cols])
        rate_scale, gain = vectors[2:3], vectors[3:4]
        x = jnp.where(own, xk_ref[:, cols], xr_ref[:, cols])
        normed = (x.astype(F32) * widen(inv_ref[...], width) * gain).astype(BF16)
        normed_ref[:, cols] = normed
        rate_weight = jnp.where(own, wk_ref[head], wr_ref[head])
        input_weight = jnp.where(own, wk_ref[heads + head], wr_ref[heads + head])
        prer_ref[...] = contract(normed, rate_weight, (1, 0)) + vectors[0:1]
        prei_ref[...] = contract(normed, input_weight, (1, 0)) + vectors[1:2]

        def per_micro(m, _):
            base = pl.multiple_of(m * tok_rows, tok_rows)
            state = jnp.zeros((8, width), F32)
            product = jnp.ones((8, width), F32)
            for pair in range(tok_rows // 16):
                rows = pl.ds(base + 16 * pair, 16)
                x_norm = normed_ref[rows, cols].astype(F32)
                keep = widen(open_ref[rows, :], width)
                rate_gate = 1.0 / (1.0 + jnp.exp(-prer_ref[rows, :]))
                input_gate = 1.0 / (1.0 + jnp.exp(-prei_ref[rows, :]))
                log_decay = rate_gate * rate_scale
                decay = jnp.exp(log_decay)
                square_gap = decay * decay
                twice = 2.0 * log_decay
                small = -twice * (
                    1.0 + twice * (1 / 2 + twice * (1 / 6 + twice * (1 / 24 + twice * (1 / 120))))
                )
                gap = jnp.where(twice > -0.1, small, 1.0 - square_gap)
                gap = jnp.maximum(gap, 1e-06)
                inv_mult = lax.rsqrt(gap)
                multiplier = jnp.where(keep > 0.0, gap * inv_mult, 1.0)
                decay_eff = decay * keep
                rate_slope = rate_scale * rate_gate * (1.0 - rate_gate)
                gated = input_gate * x_norm
                passed = multiplier * input_gate
                drive = passed * x_norm
                decay_ref[rows, cols] = decay_eff
                p1_ref[rows, cols] = decay_eff * rate_slope
                p2_ref[rows, cols] = keep * gated * square_gap * inv_mult * rate_slope
                p3_ref[rows, cols] = drive * (1.0 - input_gate)
                p4_ref[rows, cols] = passed
                for part in (slice(0, 8), slice(8, 16)):
                    state = decay_eff[part] * state + drive[part]
                    product = decay_eff[part] * product
            fdecay, fstate = sublane_scan(product, state, False)
            block_rows = pl.ds(pl.multiple_of(m * 8, 8), 8)
            fdecay_ref[block_rows, cols] = fdecay
            fstate_ref[block_rows, cols] = fstate
            ahead_ref[pl.ds(m, 1), cols] = fdecay[7:8]
            ahead_ref[pl.ds(micro_count + m, 1), cols] = fstate[7:8]
            if layer:
                leaving = reverse_blocks(decay_ref, up_ref, base, cols, tok_rows, width)
                rdecay, rgrad = sublane_scan(product, leaving, True)
                rgrad_ref[block_rows, cols] = rgrad
                ahead_ref[pl.ds(2 * micro_count + m, 1), cols] = rgrad[0:1]
            else:
                rdecay, _unused = sublane_scan(product, product, True)
            rdecay_ref[block_rows, cols] = rdecay
            return 0

        lax.fori_loop(0, micro_count, per_micro, 0)
        return 0

    lax.fori_loop(0, heads, per_head, 0)


def late_kernel(
    micro_count, tok_rows, full_width, cross_count, seq_at, section_at, part_ref, xk_ref, xr_ref,
    inv_ref, factor_ref, ahead_ref, *refs
):
    crosses = refs[:cross_count]
    early_ref, rgrad_ref, pay_ref, scale_ref = refs[cross_count:]
    decay_ref = factor_ref.at[0]
    width = 256
    column = to_column([part[...] for part in crosses]) / full_width
    inv = inv_ref[...]
    scale_ref[...] = inv * inv * inv * column
    own = section_at[0] == 1

    def per_head(head, _):
        cols = head_columns(head, width)

        def per_micro(m, _):
            base = pl.multiple_of(m * tok_rows, tok_rows)
            carry = jnp.zeros((8, width), F32)
            product = jnp.ones((8, width), F32)
            for pair in reversed(range(tok_rows // 16)):
                rows = pl.ds(base + 16 * pair, 16)
                decay = decay_ref[rows, cols]
                x = jnp.where(own, xk_ref[rows, cols], xr_ref[rows, cols]).astype(F32)
                scale = widen(scale_ref[rows, :], width)
                early = (part_ref[rows, cols] - x * scale).astype(BF16)
                early_ref[rows, cols] = early
                upstream = early.astype(F32)
                carry = decay[8:] * (upstream[8:] + carry)
                carry = decay[:8] * (upstream[:8] + carry)
                product = product * decay[8:] * decay[:8]
            _, rgrad = sublane_scan(product, carry, True)
            rgrad_ref[pl.ds(pl.multiple_of(m * 8, 8), 8), cols] = rgrad
            pay_ref[pl.ds(2 * micro_count + m, 1), cols] = rgrad[0:1]
            return 0

        lax.fori_loop(0, micro_count, per_micro, 0)
        return 0

    pay_ref[: 2 * micro_count, :] = ahead_ref[...]
    lax.fori_loop(0, part_ref.shape[1] // width, per_head, 0)


def backward_kernel(
    micro_count, tok_rows, seq_count, layer, direct, pay_count, seq_at, section_at, *refs
):
    pays = refs[:pay_count]
    (
        xk_ref, xr_ref, up_ref, normed_ref, factor_ref, block_ref, rgrad_ref, inv_ref,
        vk_ref, vr_ref, wk_ref, wr_ref, _before,
        part_ref, cross_ref, *unit_refs,
        enter_ref, leave_ref, slope_ref, direct_ref, gr_ref, gi_ref, fold_ref, weight_ref,
    ) = refs[pay_count:]
    decay_ref, p1_ref, p2_ref, p3_ref, p4_ref = (factor_ref.at[k] for k in range(5))
    fdecay_ref, fstate_ref, rdecay_ref = (block_ref.at[k] for k in range(3))
    width = wk_ref.shape[2]
    heads = xk_ref.shape[1] // width
    rank = seq_at[0]
    micro = micro_count
    own = section_at[0] == layer
    decays, states, grads = (slice(k * micro, (k + 1) * micro) for k in range(3))
    state_in = jnp.zeros(enter_ref.shape, F32)
    grad_in = jnp.zeros(leave_ref.shape, F32)
    if direct:
        near, far = pays[0][...], pays[1][...]
        late = jnp.bitwise_and(rank, 2) > 0
        odd = jnp.bitwise_and(rank, 1) > 0
        state_in = jnp.where(late, far, state_in)
        state_in = jnp.where(odd, near[states] + near[decays] * state_in, state_in)
        grad_in = jnp.where(late, grad_in, far)
        grad_in = jnp.where(odd, grad_in, near[grads] + near[decays] * grad_in)
    else:
        for at in range(seq_count - 1):
            pay = pays[0][at]
            state_in = jnp.where(at < rank, pay[states] + pay[decays] * state_in, state_in)
        for at in reversed(range(1, seq_count)):
            pay = pays[0][at]
            grad_in = jnp.where(at > rank, pay[grads] + pay[decays] * grad_in, grad_in)
    enter_ref[...] = state_in
    leave_ref[...] = grad_in
    fold_ref[...] = jnp.zeros(fold_ref.shape, F32)

    sub = lax.broadcasted_iota(jnp.int32, (8, width), 0)
    zero = jnp.zeros((8, width), F32)

    def per_head(head, _):
        cols = head_columns(head, width)

        def per_micro(m, sums):
            sum_rate, sum_input = sums
            base = pl.multiple_of(m * tok_rows, tok_rows)
            block_rows = pl.ds(pl.multiple_of(m * 8, 8), 8)
            enter = enter_ref[pl.ds(m, 1), cols]
            leave = leave_ref[pl.ds(m, 1), cols]
            after = fstate_ref[block_rows, cols] + fdecay_ref[block_rows, cols] * enter
            state = jnp.where(sub == 0, enter, pltpu.roll(after, 1, 0))
            before = rgrad_ref[block_rows, cols] + rdecay_ref[block_rows, cols] * leave
            carry = jnp.where(sub == 7, leave, pltpu.roll(before, 7, 0))
            for pair in range(tok_rows // 16):
                rows = pl.ds(base + 16 * pair, 16)
                decay = decay_ref[rows, cols]
                drive = p4_ref[rows, cols] * normed_ref[rows, cols].astype(F32)
                middle = decay[:8] * state + drive[:8]
                previous = jnp.concatenate([state, middle], axis=0)
                state = decay[8:] * middle + drive[8:]
                slope_ref[pl.ds(16 * pair, 16), :] = (
                    previous * p1_ref[rows, cols] - p2_ref[rows, cols]
                )
            for pair in reversed(range(tok_rows // 16)):
                rows = pl.ds(base + 16 * pair, 16)
                decay = decay_ref[rows, cols]
                upstream = up_ref[rows, cols].astype(F32)
                late = upstream[8:] + carry
                early = upstream[:8] + decay[8:] * late
                carry = decay[:8] * early
                grad = jnp.concatenate([early, late], axis=0)
                grad_rate = (grad * slope_ref[pl.ds(16 * pair, 16), :]).astype(BF16)
                grad_input = (grad * p3_ref[rows, cols]).astype(BF16)
                gr_ref[rows, :] = grad_rate
                gi_ref[rows, :] = grad_input
                direct_ref[rows, :] = grad * p4_ref[rows, cols]
                wide_rate = grad_rate.astype(F32)
                wide_input = grad_input.astype(F32)
                sum_rate = sum_rate + wide_rate[:8] + wide_rate[8:]
                sum_input = sum_input + wide_input[:8] + wide_input[8:]
            return sum_rate, sum_input

        sum_rate, sum_input = lax.fori_loop(0, micro, per_micro, (zero, zero))

        normed = normed_ref[:, cols]
        places = [jnp.bitwise_xor(2 * head + gate, rank if direct else 0) for gate in range(2)]
        for place, grad_ref in zip(places, (gr_ref, gi_ref)):
            unit_ref = weight_ref.at[place]
            unit_ref[:width, :] = contract(normed, grad_ref[...], (0, 0)).astype(BF16)
        rate_weight = jnp.where(own, wk_ref[head], wr_ref[head])
        input_weight = jnp.where(own, wk_ref[heads + head], wr_ref[heads + head])
        direct_ref[...] += contract(gr_ref[...], rate_weight, (1, 1)) + contract(
            gi_ref[...], input_weight, (1, 1)
        )
        gain = jnp.where(own, vk_ref[3:4, cols], vr_ref[3:4, cols])

        def per_part(m, sum_gain):
            rows = pl.ds(pl.multiple_of(m * tok_rows, tok_rows), tok_rows)
            inv = widen(inv_ref[rows, :], width)
            x = jnp.where(own, xk_ref[rows, cols], xr_ref[rows, cols]).astype(F32)
            grad_normed = direct_ref[rows, :]
            scaled = grad_normed * gain
            part_ref[rows, cols] = up_ref[rows, cols].astype(F32) + inv * scaled
            weighted = grad_normed * x * inv
            fold_ref[rows, :] += fold_lanes(x * scaled)
            for at in range(0, tok_rows, 8):
                sum_gain = sum_gain + weighted[at : at + 8]
            return sum_gain

        sum_gain = lax.fori_loop(0, micro, per_part, zero)
        vector = jnp.concatenate(
            [
                jnp.sum(sum_rate, axis=0, keepdims=True),
                jnp.sum(sum_input, axis=0, keepdims=True),
                jnp.sum(sum_gain, axis=0, keepdims=True),
                jnp.zeros((VECTOR_ROWS - 3, width), F32),
            ],
            axis=0,
        )
        high = vector.astype(BF16)
        weight_ref[places[0], width:, :] = high
        weight_ref[places[1], width:, :] = (vector - high.astype(F32)).astype(BF16)
        return 0

    lax.fori_loop(0, heads, per_head, 0)
    cross_ref[...] = to_row(fold_ref[...])
    if not direct:
        unit_refs[0][...] = weight_ref[...]
    elif layer:
        keep_ref, send_ref = unit_refs
        for k in range(4):
            (send_ref if k % 2 else keep_ref)[k // 2] = weight_ref[k]
    else:
        for k, unit_ref in enumerate(unit_refs):
            unit_ref[...] = weight_ref[k]


def last_kernel(
    full_width, tok_rows, cross_count, section_at, part_ref, xk_ref, xr_ref, inv_ref, early_ref,
    *refs
):
    column = to_column([part[...] for part in refs[:cross_count]]) / full_width
    keep_ref, send_ref = refs[cross_count:]
    inv = inv_ref[...]
    scale = inv * inv * inv * column
    order = row_order(xk_ref.shape[0], tok_rows).astype(BF16)
    bottom = section_at[0] == 0
    for at in range(0, xk_ref.shape[1], 256):
        cols = slice(at, at + 256)
        x = jnp.where(bottom, xk_ref[:, cols], xr_ref[:, cols]).astype(F32)
        value = (part_ref[:, cols] - x * widen(scale, 256)).astype(BF16)
        early = early_ref[:, cols]
        keep_ref[:, cols] = contract(order, jnp.where(bottom, value, early), (0, 0)).astype(BF16)
        send_ref[:, cols] = contract(order, jnp.where(bottom, early, value), (0, 0)).astype(BF16)


def join_kernel(section_at, keep_ref, arrived_ref, out_ref):
    half = keep_ref.shape[1]
    mine = section_at[0] * half
    out_ref[:, pl.ds(pl.multiple_of(mine, 128), half)] = keep_ref[...]
    out_ref[:, pl.ds(pl.multiple_of(half - mine, 128), half)] = arrived_ref[...]


def add_kernel(*refs):
    total = refs[0][...].astype(F32)
    for part in refs[1:-1]:
        total = total + part[...].astype(F32)
    refs[-1][...] = total.astype(refs[-1].dtype)


def add_pairs_kernel(a_ref, b_ref, *outs):
    for k, out_ref in enumerate(outs):
        out_ref[...] = (a_ref[k].astype(F32) + b_ref[k].astype(F32)).astype(out_ref.dtype)


def weights_kernel(units, scale, section_at, unit_at, *refs):
    tops, lows, others = refs[:units], refs[units : 2 * units], refs[2 * units : 3 * units]
    rate_ref, input_ref, vector_ref, ordered_ref, wide_ref, rows_ref, sems = refs[3 * units :]
    size = rate_ref.shape[1]
    half_heads = units // 2
    section = section_at[0]
    mine = section * units
    for k in range(units):
        place = jnp.bitwise_xor(unit_at[0], k)
        ordered_ref[mine + place] = jnp.where(section == 1, tops[k][...], lows[k][...])
        ordered_ref[units - mine + place] = others[k][...]
    copies = []
    for index in range(2 * units):
        head, gate = index // 2, index % 2
        wide_ref[index] = ordered_ref[index, :size, :].astype(F32) * scale
        target = (rate_ref, input_ref)[gate].at[head]
        copies.append(pltpu.make_async_copy(wide_ref.at[index], target, sems.at[index]))
        copies[-1].start()
    for head in range(2 * half_heads):
        rows = ordered_ref[2 * head, size:, :].astype(F32)
        rows = rows + ordered_ref[2 * head + 1, size:, :].astype(F32)
        for k in range(3):
            rows_ref[k, :, head * size : (head + 1) * size] = rows[k : k + 1] * scale
    copies.append(pltpu.make_async_copy(rows_ref, vector_ref, sems.at[2 * units]))
    copies[-1].start()
    for copy in copies:
        copy.wait()


def xor_moves(value, axis, k):
    return lax.ppermute(value, axis, [(i, i ^ k) for i in range(lax.axis_size(axis))])


def swap_sections(value):
    return lax.ppermute(value, "section", [(0, 1), (1, 0)])


def chan_parts(value):
    count = lax.axis_size("chan")
    if count & (count - 1):
        gathered = lax.all_gather(value, "chan")
        return [gathered[k] for k in range(count)]
    return [xor_moves(value, "chan", k) for k in reversed(range(1, count))] + [value]


def seq_pays(pay, seq_at, micro):
    if lax.axis_size("seq") != DIRECT_RANKS:
        return [lax.all_gather(pay, "seq")]
    near = xor_moves(pay, "seq", 1)
    ends = pl.pallas_call(
        functools.partial(pair_ends_kernel, micro),
        in_specs=[
            pl.BlockSpec(memory_space=pltpu.SMEM),
            pl.BlockSpec(memory_space=pltpu.VMEM),
            pl.BlockSpec(memory_space=pltpu.VMEM),
        ],
        out_shape=jax.ShapeDtypeStruct((micro, pay.shape[1]), F32),
        compiler_params=params(),
        cost_estimate=cost(0, 8 * pay.size),
    )(seq_at, pay, near)
    return [near, xor_moves(ends, "seq", 2)]


def add_units(value, *others):
    return pl.pallas_call(
        add_kernel,
        out_shape=jax.ShapeDtypeStruct(value.shape, value.dtype),
        compiler_params=params(),
        cost_estimate=cost(0, 8 * value.size),
    )(value, *others)


def add_pairs(a, b):
    return pl.pallas_call(
        add_pairs_kernel,
        out_shape=[jax.ShapeDtypeStruct(a.shape[1:], a.dtype)] * a.shape[0],
        compiler_params=params(),
        cost_estimate=cost(0, 6 * a.size),
    )(a, b)


def after(value, *others):
    return lax.optimization_barrier((value, *others))[0]


def on_device(
    layer_inputs,
    out_grad,
    rate_weight,
    input_weight,
    rate_bias,
    input_bias,
    decay_param,
    norm_gain,
    doc_starts,
):
    micro, tok_rows, chan_width = out_grad.shape
    seq_count = lax.axis_size("seq")
    heads, size = rate_weight.shape[1:3]
    half_heads = heads // 2
    half = chan_width // 2
    rows = micro * tok_rows
    full_width = chan_width * lax.axis_size("chan")
    grad_scale = 1.0 / math.sqrt(micro * tok_rows * seq_count)
    seq_at = lax.axis_index("seq").reshape(1).astype(jnp.int32)
    section = lax.axis_index("section")
    section_at = section.reshape(1).astype(jnp.int32)

    x_raw = layer_inputs.reshape(rows, chan_width)
    up_raw = out_grad.reshape(rows, chan_width)

    def shape(dims, dtype=F32):
        return jax.ShapeDtypeStruct(dims, dtype)

    smem = pl.BlockSpec(memory_space=pltpu.SMEM)
    whole = pl.BlockSpec(memory_space=pltpu.VMEM)

    def call(kernel, scalars, arrays, outs, scratch=(), flops=0, size_bytes=0, specs=None):
        return pl.pallas_call(
            kernel,
            in_specs=[smem] * len(scalars) + (specs or [whole] * len(arrays)),
            out_shape=outs,
            scratch_shapes=[
                pltpu.VMEM(*entry) if isinstance(entry, tuple) else entry for entry in scratch
            ],
            compiler_params=params(),
            cost_estimate=cost(flops, size_bytes),
        )(*scalars, *arrays)

    half_x = shape((rows, half), BF16)
    half_w = shape((heads, size, size), BF16)
    half_v = shape((8, half))
    square, x_keep, x_send, upstream, w_keep, w_send, v_keep, v_send, opened = call(
        functools.partial(prepare_kernel, micro, tok_rows),
        [section_at, seq_at],
        [
            pltpu.with_memory_space_constraint(array, pltpu.HBM)
            for array in (
                doc_starts, x_raw, up_raw, rate_weight[0], input_weight[0],
                rate_bias, input_bias, decay_param, norm_gain,
            )
        ],
        [shape((8, rows)), half_x, half_x, half_x, half_w, half_w, half_v, half_v, shape((rows, 128))],
        [
            (doc_starts.shape, jnp.int32),
            ((rows, chan_width), BF16),
            ((rows, half), BF16),
            ((4, 1, chan_width), F32),
            pltpu.SemaphoreType.DMA((11,)),
        ],
        specs=[pl.BlockSpec(memory_space=pltpu.HBM)] * 9,
        flops=4 * rows * rows * chan_width,
        size_bytes=12 * rows * chan_width,
    )
    own_squares = chan_parts(square)
    other_squares = swap_sections(add_units(*own_squares))
    x_got, w_got, v_got = (swap_sections(value) for value in (x_send, w_send, v_send))

    big = shape((rows, half))
    blocks = shape((micro * 8, half))

    def forward(layer, beside):
        return call(
            functools.partial(
                forward_kernel, micro, tok_rows, full_width, layer, len(own_squares)
            ),
            [seq_at, section_at],
            [
                *own_squares, other_squares, opened, x_keep, x_got, w_keep, w_got, v_keep, v_got,
                beside,
            ],
            [
                half_x,
                shape((5, rows, half)),
                shape((3, micro * 8, half)),
                shape(((2 + layer) * micro, half)),
                shape((rows, 128)),
            ]
            + [blocks] * layer,
            [((rows, size), F32)] * 2,
            flops=4 * rows * size * half,
            size_bytes=24 * rows * half,
        )

    direct = seq_count == DIRECT_RANKS and heads == DIRECT_RANKS
    unit_dims = {0: [()] * 4, 1: [(2,)] * 2} if direct else {0: [(heads,)], 1: [(heads,)]}

    def backward(layer, pays, upstream, kept, rgrad, before):
        normed, factors, block, _, inv = kept
        return call(
            functools.partial(
                backward_kernel, micro, tok_rows, seq_count, layer, direct, len(pays)
            ),
            [seq_at, section_at],
            [
                *pays, x_keep, x_got, upstream, normed, factors, block, rgrad, inv,
                v_keep, v_got, w_keep, w_got, before,
            ],
            [big, shape((8, rows))]
            + [shape(dims + (size + VECTOR_ROWS, size), BF16) for dims in unit_dims[layer]],
            [
                ((micro, half), F32),
                ((micro, half), F32),
                ((tok_rows, size), F32),
                ((rows, size), F32),
                ((rows, size), BF16),
                ((rows, size), BF16),
                ((rows, 128), F32),
                ((heads, size + VECTOR_ROWS, size), BF16),
            ],
            flops=8 * rows * size * half,
            size_bytes=30 * rows * half,
        )

    def chip_sum(value):
        return add_units(value, swap_sections(value))

    *top, top_rgrad = forward(1, upstream)
    pays = seq_pays(top[3], seq_at, micro)
    low = forward(0, top[1])
    part, cross, *top_parts = backward(1, pays, upstream, top, top_rgrad, low[3])
    cross = chip_sum(cross)
    parts = chan_parts(cross)
    if direct:
        top_parts[1] = after(top_parts[1], cross)
        arrived = xor_moves(top_parts[1], "seq", 1)
    early, low_rgrad, low_pay = call(
        functools.partial(late_kernel, micro, tok_rows, full_width, len(parts)),
        [seq_at, section_at],
        [part, x_keep, x_got, top[4], low[1], low[3], *parts],
        [half_x, blocks, shape((3 * micro, half))],
        [((rows, 128), F32)],
        flops=8 * rows * half,
        size_bytes=12 * rows * half,
    )
    pays = seq_pays(low_pay, seq_at, micro)
    if direct:
        own_pair, far_pair = add_pairs(top_parts[0], after(arrived, pays[0]))
        arrived = xor_moves(far_pair, "seq", 2)
        top_own = add_units(own_pair, after(arrived, *pays))
        top_far = xor_moves(top_own, "seq", 2)
    part, cross, *low_parts = backward(
        0, pays, early, low, low_rgrad, top_own if direct else low_pay
    )
    parts = chan_parts(after(chip_sum(cross), top_far) if direct else chip_sum(cross))
    if direct:
        place = lax.axis_index("seq")
        low_arrived = [xor_moves(low_parts[k], "seq", k) for k in (3, 2, 1)]
        low_arrived, parts = lax.optimization_barrier((low_arrived, parts))
        low_own = add_units(low_parts[0], *low_arrived)
        low_units = [low_own] + [xor_moves(low_own, "seq", k) for k in (1, 2, 3)]
        top_near = xor_moves(top_own, "seq", 1)
        top_last = xor_moves(top_far, "seq", 1)
        top_units = [top_own, top_near, top_far, top_last]
    else:
        place = jnp.zeros((), jnp.int32)
        top_units, low_units = (
            [total[k] for k in range(heads)]
            for total in (
                lax.psum(value.astype(F32), "seq").astype(BF16)
                for value in (top_parts[0], low_parts[0])
            )
        )
    grads_keep, grads_send = call(
        functools.partial(last_kernel, full_width, tok_rows, len(parts)),
        [section_at],
        [part, x_keep, x_got, low[4], early, *parts],
        [half_x, half_x],
        flops=4 * rows * rows * half,
        size_bytes=12 * rows * half,
    )
    grads = call(
        join_kernel, [section_at], [grads_keep, swap_sections(grads_send)],
        shape((rows, chan_width), BF16), size_bytes=4 * rows * chan_width,
    )

    other_units = [
        swap_sections(jnp.where(section == 1, b, a)) for a, b in zip(top_units, low_units)
    ]
    rate_total, input_total, vector = pl.pallas_call(
        functools.partial(weights_kernel, heads, grad_scale),
        in_specs=[smem, smem] + [whole] * (3 * heads),
        out_specs=[pl.BlockSpec(memory_space=pltpu.HBM)] * 3,
        out_shape=[
            shape((heads, size, size)),
            shape((heads, size, size)),
            shape((3, 1, chan_width)),
        ],
        scratch_shapes=[
            pltpu.VMEM((2 * heads, size + VECTOR_ROWS, size), BF16),
            pltpu.VMEM((2 * heads, size, size), F32),
            pltpu.VMEM((3, 1, chan_width), F32),
            pltpu.SemaphoreType.DMA((2 * heads + 1,)),
        ],
        compiler_params=params(),
        cost_estimate=cost(0, 8 * heads * size * size),
    )(
        section_at, place.reshape(1).astype(jnp.int32), *top_units, *low_units, *other_units
    )
    return (
        grads.reshape(1, micro, tok_rows, chan_width),
        rate_total[None],
        input_total[None],
        jnp.swapaxes(vector, 0, 1),
    )


def solution(mesh):
    in_specs = (
        P("section", None, "seq", "chan"),
        P(None, "seq", "chan"),
        P("section", "chan", None, None),
        P("section", "chan", None, None),
        P("section", "chan"),
        P("section", "chan"),
        P("section", "chan"),
        P("section", "chan"),
        P(),
    )
    out_specs = (
        P("section", None, "seq", "chan"),
        P("section", "chan", None, None),
        P("section", "chan", None, None),
        P("section", None, "chan"),
    )
    return jax.shard_map(
        on_device, mesh=mesh, in_specs=in_specs, out_specs=out_specs, check_vma=False
    )
```

```python
import functools
import math

import jax
import jax.numpy as jnp
from jax import lax
from jax.experimental import pallas as pl
from jax.experimental.pallas import tpu as pltpu
from jax.sharding import PartitionSpec as P

F32 = jnp.float32
BF16 = jnp.bfloat16
HIGH = lax.Precision.HIGHEST
VECTOR_ROWS = 16
DIRECT_RANKS = 4


def params(limit=8):
    return pltpu.CompilerParams(vmem_limit_bytes=limit * 1024 * 1024)


def cost(flops, size):
    return pl.CostEstimate(flops=flops, bytes_accessed=size, transcendentals=0)


def contract(a, b, dims, precision=None):
    return lax.dot_general(
        a, b, ((dims[:1], dims[1:]), ((), ())), precision=precision, preferred_element_type=F32
    )


def row_order(rows, tok_rows):
    shift = tok_rows.bit_length() - 1
    at = lax.broadcasted_iota(jnp.int32, (rows, rows), 0)
    source = lax.broadcasted_iota(jnp.int32, (rows, rows), 1)
    inner = jnp.bitwise_and(at, tok_rows - 1)
    wanted = (
        jnp.left_shift(jnp.right_shift(at, shift), shift)
        + jnp.bitwise_and(inner, 7) * (tok_rows // 8)
        + jnp.right_shift(inner, 3)
    )
    return jnp.where(wanted == source, 1.0, 0.0).astype(F32)


def to_column(parts):
    total = parts[0]
    for part in parts[1:]:
        total = total + part
    return contract(total, jnp.full((8, 128), 0.125, F32), (0, 0), HIGH)


def to_row(folded):
    return contract(jnp.ones((8, folded.shape[1]), F32), folded, (1, 1), HIGH)


def fold_lanes(value):
    total = value[:, :128]
    for at in range(128, value.shape[1], 128):
        total = total + value[:, at : at + 128]
    return total


def widen(column, width):
    return jnp.concatenate([column] * (width // 128), axis=1)


def prepare_kernel(
    micro_count, tok_rows, section_at, seq_at, raw_starts, raw_x_ref, up_ref, rw_ref, iw_ref,
    rb_ref, ib_ref, dp_ref, gain_ref, square_ref, xk_ref, xs_ref, upp_ref, wk_ref, ws_ref,
    vk_ref, vs_ref, open_ref, starts, x_ref, raw_up_ref, raw_ref, sems,
):
    half = x_ref.shape[1] // 2
    heads = rw_ref.shape[0] // 2
    section = section_at[0]

    def columns(side):
        return pl.ds(pl.multiple_of(side * half, 128), half)

    moves = [(raw_x_ref, x_ref), (raw_starts, starts), (up_ref.at[:, columns(section)], raw_up_ref)]
    moves += [
        (source, raw_ref.at[k]) for k, source in enumerate((rb_ref, ib_ref, dp_ref, gain_ref))
    ]
    for side, w_out in ((section, wk_ref), (1 - section, ws_ref)):
        picked = pl.ds(side * heads, heads)
        moves += [
            (rw_ref.at[picked], w_out.at[pl.ds(0, heads)]),
            (iw_ref.at[picked], w_out.at[pl.ds(heads, heads)]),
        ]
    copies = [
        pltpu.make_async_copy(source, target, sems.at[k])
        for k, (source, target) in enumerate(moves)
    ]
    for copy in copies:
        copy.start()
    order = row_order(x_ref.shape[0], tok_rows).astype(BF16)
    copies[0].wait()
    total = None
    for side, x_out in ((section, xk_ref), (1 - section, xs_ref)):
        x = contract(order, x_ref[:, columns(side)], (1, 0))
        x_out[...] = x.astype(BF16)
        part = fold_lanes(x * x)
        total = part if total is None else total + part
    square_ref[...] = to_row(total)
    for copy in copies[1:]:
        copy.wait()
    upp_ref[...] = contract(order, raw_up_ref[...], (1, 0)).astype(BF16)
    for side, v_out in ((section, vk_ref), (1 - section, vs_ref)):
        rate_bias, input_bias, decay_param, gain = (
            raw_ref[k, :, columns(side)] for k in range(4)
        )
        slow = -decay_param
        soft = jnp.maximum(slow, 0.0) + jnp.log1p(jnp.exp(-jnp.abs(slow)))
        v_out[...] = jnp.concatenate(
            [rate_bias, input_bias, -8.0 * soft, gain, jnp.zeros((4, half), F32)], axis=0
        )
    shift = tok_rows.bit_length() - 1
    at = lax.broadcasted_iota(jnp.int32, open_ref.shape, 0)
    inner = jnp.bitwise_and(at, tok_rows - 1)
    micro = jnp.right_shift(at, shift)
    position = (
        seq_at[0] * tok_rows
        + jnp.bitwise_and(inner, 7) * (tok_rows // 8)
        + jnp.right_shift(inner, 3)
    )
    reset = position == 0
    for m in range(micro_count):
        for d in range(starts.shape[1]):
            hit = jnp.logical_and(micro == m, position == starts[m : m + 1, d : d + 1])
            reset = jnp.logical_or(reset, hit)
    open_ref[...] = jnp.where(reset, 0.0, 1.0)


def sublane_scan(decay, value, reverse):
    at = lax.broadcasted_iota(jnp.int32, decay.shape, 0)
    for step in (1, 2, 4):
        shift = 8 - step if reverse else step
        inside = at < 8 - step if reverse else at >= step
        value_far = pltpu.roll(value, shift, 0)
        decay_far = pltpu.roll(decay, shift, 0)
        value = jnp.where(inside, value + decay * value_far, value)
        decay = jnp.where(inside, decay * decay_far, decay)
    return decay, value


def reverse_blocks(decay_ref, up_ref, base, cols, tok_rows, width):
    carry = jnp.zeros((8, width), F32)
    for pair in reversed(range(tok_rows // 16)):
        rows = pl.ds(base + 16 * pair, 16)
        decay = decay_ref[rows, cols]
        upstream = up_ref[rows, cols].astype(F32)
        carry = decay[8:] * (upstream[8:] + carry)
        carry = decay[:8] * (upstream[:8] + carry)
    return carry


def pair_ends_kernel(micro, seq_at, own_ref, near_ref, out_ref):
    own, near = own_ref[...], near_ref[...]
    odd = jnp.bitwise_and(seq_at[0], 1) == 1
    first = jnp.where(odd, near, own)
    last = jnp.where(odd, own, near)
    state = last[micro : 2 * micro] + last[:micro] * first[micro : 2 * micro]
    grad = first[2 * micro :] + first[:micro] * last[2 * micro :]
    out_ref[...] = jnp.where(jnp.bitwise_and(seq_at[0], 2) == 0, state, grad)


def head_columns(head, width):
    return pl.ds(pl.multiple_of(head * width, width), width)


def forward_kernel(micro_count, tok_rows, full_width, layer, square_count, seq_at, section_at, *refs):
    own_squares, other_squares = refs[:square_count], refs[square_count]
    refs = refs[square_count + 1 :]
    open_ref, xk_ref, xr_ref, wk_ref, wr_ref, vk_ref, vr_ref = refs[:7]
    refs = refs[7:]
    if layer:
        up_ref, *refs = refs
    else:
        _above, *refs = refs
    normed_ref, factor_ref, block_ref, ahead_ref, inv_ref, *refs = refs
    decay_ref, p1_ref, p2_ref, p3_ref, p4_ref = (factor_ref.at[k] for k in range(5))
    fdecay_ref, fstate_ref, rdecay_ref = (block_ref.at[k] for k in range(3))
    if layer:
        rgrad_ref, *refs = refs
    prer_ref, prei_ref = refs
    width = wk_ref.shape[2]
    heads = xk_ref.shape[1] // width
    own = section_at[0] == layer

    total = jnp.where(own, sum(part[...] for part in own_squares), other_squares[...])
    inv_ref[...] = lax.rsqrt(to_column([total]) / full_width + 1e-06)

    def per_head(head, _):
        cols = head_columns(head, width)
        vectors = jnp.where(own, vk_ref[:, cols], vr_ref[:, cols])
        rate_scale, gain = vectors[2:3], vectors[3:4]
        x = jnp.where(own, xk_ref[:, cols], xr_ref[:, cols])
        normed = (x.astype(F32) * widen(inv_ref[...], width) * gain).astype(BF16)
        normed_ref[:, cols] = normed
        rate_weight = jnp.where(own, wk_ref[head], wr_ref[head])
        input_weight = jnp.where(own, wk_ref[heads + head], wr_ref[heads + head])
        prer_ref[...] = contract(normed, rate_weight, (1, 0)) + vectors[0:1]
        prei_ref[...] = contract(normed, input_weight, (1, 0)) + vectors[1:2]

        def per_micro(m, _):
            base = pl.multiple_of(m * tok_rows, tok_rows)
            state = jnp.zeros((8, width), F32)
            product = jnp.ones((8, width), F32)
            for pair in range(tok_rows // 16):
                rows = pl.ds(base + 16 * pair, 16)
                x_norm = normed_ref[rows, cols].astype(F32)
                keep = widen(open_ref[rows, :], width)
                rate_gate = 1.0 / (1.0 + jnp.exp(-prer_ref[rows, :]))
                input_gate = 1.0 / (1.0 + jnp.exp(-prei_ref[rows, :]))
                log_decay = rate_gate * rate_scale
                decay = jnp.exp(log_decay)
                square_gap = decay * decay
                twice = 2.0 * log_decay
                small = -twice * (
                    1.0 + twice * (1 / 2 + twice * (1 / 6 + twice * (1 / 24 + twice * (1 / 120))))
                )
                gap = jnp.where(twice > -0.1, small, 1.0 - square_gap)
                gap = jnp.maximum(gap, 1e-06)
                inv_mult = lax.rsqrt(gap)
                multiplier = jnp.where(keep > 0.0, gap * inv_mult, 1.0)
                decay_eff = decay * keep
                rate_slope = rate_scale * rate_gate * (1.0 - rate_gate)
                gated = input_gate * x_norm
                passed = multiplier * input_gate
                drive = passed * x_norm
                decay_ref[rows, cols] = decay_eff
                p1_ref[rows, cols] = decay_eff * rate_slope
                p2_ref[rows, cols] = keep * gated * square_gap * inv_mult * rate_slope
                p3_ref[rows, cols] = drive * (1.0 - input_gate)
                p4_ref[rows, cols] = passed
                for part in (slice(0, 8), slice(8, 16)):
                    state = decay_eff[part] * state + drive[part]
                    product = decay_eff[part] * product
            fdecay, fstate = sublane_scan(product, state, False)
            block_rows = pl.ds(pl.multiple_of(m * 8, 8), 8)
            fdecay_ref[block_rows, cols] = fdecay
            fstate_ref[block_rows, cols] = fstate
            ahead_ref[pl.ds(m, 1), cols] = fdecay[7:8]
            ahead_ref[pl.ds(micro_count + m, 1), cols] = fstate[7:8]
            if layer:
                leaving = reverse_blocks(decay_ref, up_ref, base, cols, tok_rows, width)
                rdecay, rgrad = sublane_scan(product, leaving, True)
                rgrad_ref[block_rows, cols] = rgrad
                ahead_ref[pl.ds(2 * micro_count + m, 1), cols] = rgrad[0:1]
            else:
                rdecay, _unused = sublane_scan(product, product, True)
            rdecay_ref[block_rows, cols] = rdecay
            return 0

        lax.fori_loop(0, micro_count, per_micro, 0)
        return 0

    lax.fori_loop(0, heads, per_head, 0)


def late_kernel(
    micro_count, tok_rows, full_width, cross_count, seq_at, section_at, part_ref, xk_ref, xr_ref,
    inv_ref, factor_ref, ahead_ref, *refs
):
    crosses = refs[:cross_count]
    early_ref, rgrad_ref, pay_ref, scale_ref = refs[cross_count:]
    decay_ref = factor_ref.at[0]
    width = 256
    column = to_column([part[...] for part in crosses]) / full_width
    inv = inv_ref[...]
    scale_ref[...] = inv * inv * inv * column
    own = section_at[0] == 1

    def per_head(head, _):
        cols = head_columns(head, width)

        def per_micro(m, _):
            base = pl.multiple_of(m * tok_rows, tok_rows)
            carry = jnp.zeros((8, width), F32)
            product = jnp.ones((8, width), F32)
            for pair in reversed(range(tok_rows // 16)):
                rows = pl.ds(base + 16 * pair, 16)
                decay = decay_ref[rows, cols]
                x = jnp.where(own, xk_ref[rows, cols], xr_ref[rows, cols]).astype(F32)
                scale = widen(scale_ref[rows, :], width)
                early = (part_ref[rows, cols] - x * scale).astype(BF16)
                early_ref[rows, cols] = early
                upstream = early.astype(F32)
                carry = decay[8:] * (upstream[8:] + carry)
                carry = decay[:8] * (upstream[:8] + carry)
                product = product * decay[8:] * decay[:8]
            _, rgrad = sublane_scan(product, carry, True)
            rgrad_ref[pl.ds(pl.multiple_of(m * 8, 8), 8), cols] = rgrad
            pay_ref[pl.ds(2 * micro_count + m, 1), cols] = rgrad[0:1]
            return 0

        lax.fori_loop(0, micro_count, per_micro, 0)
        return 0

    pay_ref[: 2 * micro_count, :] = ahead_ref[...]
    lax.fori_loop(0, part_ref.shape[1] // width, per_head, 0)


def backward_kernel(
    micro_count, tok_rows, seq_count, layer, direct, pay_count, seq_at, section_at, *refs
):
    pays = refs[:pay_count]
    (
        xk_ref, xr_ref, up_ref, normed_ref, factor_ref, block_ref, rgrad_ref, inv_ref,
        vk_ref, vr_ref, wk_ref, wr_ref, _before,
        part_ref, cross_ref, *unit_refs,
        enter_ref, leave_ref, slope_ref, direct_ref, gr_ref, gi_ref, fold_ref, weight_ref,
    ) = refs[pay_count:]
    decay_ref, p1_ref, p2_ref, p3_ref, p4_ref = (factor_ref.at[k] for k in range(5))
    fdecay_ref, fstate_ref, rdecay_ref = (block_ref.at[k] for k in range(3))
    width = wk_ref.shape[2]
    heads = xk_ref.shape[1] // width
    rank = seq_at[0]
    micro = micro_count
    own = section_at[0] == layer
    decays, states, grads = (slice(k * micro, (k + 1) * micro) for k in range(3))
    state_in = jnp.zeros(enter_ref.shape, F32)
    grad_in = jnp.zeros(leave_ref.shape, F32)
    if direct:
        near, far = pays[0][...], pays[1][...]
        late = jnp.bitwise_and(rank, 2) > 0
        odd = jnp.bitwise_and(rank, 1) > 0
        state_in = jnp.where(late, far, state_in)
        state_in = jnp.where(odd, near[states] + near[decays] * state_in, state_in)
        grad_in = jnp.where(late, grad_in, far)
        grad_in = jnp.where(odd, grad_in, near[grads] + near[decays] * grad_in)
    else:
        for at in range(seq_count - 1):
            pay = pays[0][at]
            state_in = jnp.where(at < rank, pay[states] + pay[decays] * state_in, state_in)
        for at in reversed(range(1, seq_count)):
            pay = pays[0][at]
            grad_in = jnp.where(at > rank, pay[grads] + pay[decays] * grad_in, grad_in)
    enter_ref[...] = state_in
    leave_ref[...] = grad_in
    fold_ref[...] = jnp.zeros(fold_ref.shape, F32)

    sub = lax.broadcasted_iota(jnp.int32, (8, width), 0)
    zero = jnp.zeros((8, width), F32)

    def per_head(head, _):
        cols = head_columns(head, width)

        def per_micro(m, sums):
            sum_rate, sum_input = sums
            base = pl.multiple_of(m * tok_rows, tok_rows)
            block_rows = pl.ds(pl.multiple_of(m * 8, 8), 8)
            enter = enter_ref[pl.ds(m, 1), cols]
            leave = leave_ref[pl.ds(m, 1), cols]
            after = fstate_ref[block_rows, cols] + fdecay_ref[block_rows, cols] * enter
            state = jnp.where(sub == 0, enter, pltpu.roll(after, 1, 0))
            before = rgrad_ref[block_rows, cols] + rdecay_ref[block_rows, cols] * leave
            carry = jnp.where(sub == 7, leave, pltpu.roll(before, 7, 0))
            for pair in range(tok_rows // 16):
                rows = pl.ds(base + 16 * pair, 16)
                decay = decay_ref[rows, cols]
                drive = p4_ref[rows, cols] * normed_ref[rows, cols].astype(F32)
                middle = decay[:8] * state + drive[:8]
                previous = jnp.concatenate([state, middle], axis=0)
                state = decay[8:] * middle + drive[8:]
                slope_ref[pl.ds(16 * pair, 16), :] = (
                    previous * p1_ref[rows, cols] - p2_ref[rows, cols]
                )
            for pair in reversed(range(tok_rows // 16)):
                rows = pl.ds(base + 16 * pair, 16)
                decay = decay_ref[rows, cols]
                upstream = up_ref[rows, cols].astype(F32)
                late = upstream[8:] + carry
                early = upstream[:8] + decay[8:] * late
                carry = decay[:8] * early
                grad = jnp.concatenate([early, late], axis=0)
                grad_rate = (grad * slope_ref[pl.ds(16 * pair, 16), :]).astype(BF16)
                grad_input = (grad * p3_ref[rows, cols]).astype(BF16)
                gr_ref[rows, :] = grad_rate
                gi_ref[rows, :] = grad_input
                direct_ref[rows, :] = grad * p4_ref[rows, cols]
                wide_rate = grad_rate.astype(F32)
                wide_input = grad_input.astype(F32)
                sum_rate = sum_rate + wide_rate[:8] + wide_rate[8:]
                sum_input = sum_input + wide_input[:8] + wide_input[8:]
            return sum_rate, sum_input

        sum_rate, sum_input = lax.fori_loop(0, micro, per_micro, (zero, zero))

        normed = normed_ref[:, cols]
        places = [jnp.bitwise_xor(2 * head + gate, rank if direct else 0) for gate in range(2)]
        for place, grad_ref in zip(places, (gr_ref, gi_ref)):
            unit_ref = weight_ref.at[place]
            unit_ref[:width, :] = contract(normed, grad_ref[...], (0, 0)).astype(BF16)
        rate_weight = jnp.where(own, wk_ref[head], wr_ref[head])
        input_weight = jnp.where(own, wk_ref[heads + head], wr_ref[heads + head])
        direct_ref[...] += contract(gr_ref[...], rate_weight, (1, 1)) + contract(
            gi_ref[...], input_weight, (1, 1)
        )
        gain = jnp.where(own, vk_ref[3:4, cols], vr_ref[3:4, cols])

        def per_part(m, sum_gain):
            rows = pl.ds(pl.multiple_of(m * tok_rows, tok_rows), tok_rows)
            inv = widen(inv_ref[rows, :], width)
            x = jnp.where(own, xk_ref[rows, cols], xr_ref[rows, cols]).astype(F32)
            grad_normed = direct_ref[rows, :]
            scaled = grad_normed * gain
            part_ref[rows, cols] = up_ref[rows, cols].astype(F32) + inv * scaled
            weighted = grad_normed * x * inv
            fold_ref[rows, :] += fold_lanes(x * scaled)
            for at in range(0, tok_rows, 8):
                sum_gain = sum_gain + weighted[at : at + 8]
            return sum_gain

        sum_gain = lax.fori_loop(0, micro, per_part, zero)
        vector = jnp.concatenate(
            [
                jnp.sum(sum_rate, axis=0, keepdims=True),
                jnp.sum(sum_input, axis=0, keepdims=True),
                jnp.sum(sum_gain, axis=0, keepdims=True),
                jnp.zeros((VECTOR_ROWS - 3, width), F32),
            ],
            axis=0,
        )
        high = vector.astype(BF16)
        weight_ref[places[0], width:, :] = high
        weight_ref[places[1], width:, :] = (vector - high.astype(F32)).astype(BF16)
        return 0

    lax.fori_loop(0, heads, per_head, 0)
    cross_ref[...] = to_row(fold_ref[...])
    if not direct:
        unit_refs[0][...] = weight_ref[...]
    elif layer:
        keep_ref, send_ref = unit_refs
        for k in range(4):
            (send_ref if k % 2 else keep_ref)[k // 2] = weight_ref[k]
    else:
        for k, unit_ref in enumerate(unit_refs):
            unit_ref[...] = weight_ref[k]


def last_kernel(
    full_width, tok_rows, cross_count, section_at, part_ref, xk_ref, xr_ref, inv_ref, early_ref,
    *refs
):
    column = to_column([part[...] for part in refs[:cross_count]]) / full_width
    keep_ref, send_ref = refs[cross_count:]
    inv = inv_ref[...]
    scale = inv * inv * inv * column
    order = row_order(xk_ref.shape[0], tok_rows).astype(BF16)
    bottom = section_at[0] == 0
    for at in range(0, xk_ref.shape[1], 256):
        cols = slice(at, at + 256)
        x = jnp.where(bottom, xk_ref[:, cols], xr_ref[:, cols]).astype(F32)
        value = (part_ref[:, cols] - x * widen(scale, 256)).astype(BF16)
        early = early_ref[:, cols]
        keep_ref[:, cols] = contract(order, jnp.where(bottom, value, early), (0, 0)).astype(BF16)
        send_ref[:, cols] = contract(order, jnp.where(bottom, early, value), (0, 0)).astype(BF16)


def join_kernel(section_at, keep_ref, arrived_ref, out_ref):
    half = keep_ref.shape[1]
    mine = section_at[0] * half
    out_ref[:, pl.ds(pl.multiple_of(mine, 128), half)] = keep_ref[...]
    out_ref[:, pl.ds(pl.multiple_of(half - mine, 128), half)] = arrived_ref[...]


def add_kernel(*refs):
    total = refs[0][...].astype(F32)
    for part in refs[1:-1]:
        total = total + part[...].astype(F32)
    refs[-1][...] = total.astype(refs[-1].dtype)


def add_pairs_kernel(a_ref, b_ref, *outs):
    for k, out_ref in enumerate(outs):
        out_ref[...] = (a_ref[k].astype(F32) + b_ref[k].astype(F32)).astype(out_ref.dtype)


def weights_kernel(units, scale, section_at, unit_at, *refs):
    tops, lows, others = refs[:units], refs[units : 2 * units], refs[2 * units : 3 * units]
    rate_ref, input_ref, vector_ref, ordered_ref, wide_ref, rows_ref, sems = refs[3 * units :]
    size = rate_ref.shape[1]
    half_heads = units // 2
    section = section_at[0]
    mine = section * units
    for k in range(units):
        place = jnp.bitwise_xor(unit_at[0], k)
        ordered_ref[mine + place] = jnp.where(section == 1, tops[k][...], lows[k][...])
        ordered_ref[units - mine + place] = others[k][...]
    copies = []
    for index in range(2 * units):
        head, gate = index // 2, index % 2
        wide_ref[index] = ordered_ref[index, :size, :].astype(F32) * scale
        target = (rate_ref, input_ref)[gate].at[head]
        copies.append(pltpu.make_async_copy(wide_ref.at[index], target, sems.at[index]))
        copies[-1].start()
    for head in range(2 * half_heads):
        rows = ordered_ref[2 * head, size:, :].astype(F32)
        rows = rows + ordered_ref[2 * head + 1, size:, :].astype(F32)
        for k in range(3):
            rows_ref[k, :, head * size : (head + 1) * size] = rows[k : k + 1] * scale
    copies.append(pltpu.make_async_copy(rows_ref, vector_ref, sems.at[2 * units]))
    copies[-1].start()
    for copy in copies:
        copy.wait()


def xor_moves(value, axis, k):
    return lax.ppermute(value, axis, [(i, i ^ k) for i in range(lax.axis_size(axis))])


def swap_sections(value):
    return lax.ppermute(value, "section", [(0, 1), (1, 0)])


def chan_parts(value):
    count = lax.axis_size("chan")
    if count & (count - 1):
        gathered = lax.all_gather(value, "chan")
        return [gathered[k] for k in range(count)]
    return [xor_moves(value, "chan", k) for k in ((3, 2, 1) if count == 4 else range(1, count))] + [value]


def seq_pays(pay, seq_at, micro):
    if lax.axis_size("seq") != DIRECT_RANKS:
        return [lax.all_gather(pay, "seq")]
    near = xor_moves(pay, "seq", 1)
    ends = pl.pallas_call(
        functools.partial(pair_ends_kernel, micro),
        in_specs=[
            pl.BlockSpec(memory_space=pltpu.SMEM),
            pl.BlockSpec(memory_space=pltpu.VMEM),
            pl.BlockSpec(memory_space=pltpu.VMEM),
        ],
        out_shape=jax.ShapeDtypeStruct((micro, pay.shape[1]), F32),
        compiler_params=params(),
        cost_estimate=cost(0, 8 * pay.size),
    )(seq_at, pay, near)
    return [near, xor_moves(ends, "seq", 2)]


def add_units(value, *others):
    return pl.pallas_call(
        add_kernel,
        out_shape=jax.ShapeDtypeStruct(value.shape, value.dtype),
        compiler_params=params(),
        cost_estimate=cost(0, 8 * value.size),
    )(value, *others)


def add_pairs(a, b):
    return pl.pallas_call(
        add_pairs_kernel,
        out_shape=[jax.ShapeDtypeStruct(a.shape[1:], a.dtype)] * a.shape[0],
        compiler_params=params(),
        cost_estimate=cost(0, 6 * a.size),
    )(a, b)


def after(value, *others):
    return lax.optimization_barrier((value, *others))[0]


def on_device(
    layer_inputs,
    out_grad,
    rate_weight,
    input_weight,
    rate_bias,
    input_bias,
    decay_param,
    norm_gain,
    doc_starts,
):
    micro, tok_rows, chan_width = out_grad.shape
    seq_count = lax.axis_size("seq")
    heads, size = rate_weight.shape[1:3]
    half_heads = heads // 2
    half = chan_width // 2
    rows = micro * tok_rows
    full_width = chan_width * lax.axis_size("chan")
    grad_scale = 1.0 / math.sqrt(micro * tok_rows * seq_count)
    seq_at = lax.axis_index("seq").reshape(1).astype(jnp.int32)
    section = lax.axis_index("section")
    section_at = section.reshape(1).astype(jnp.int32)

    x_raw = layer_inputs.reshape(rows, chan_width)
    up_raw = out_grad.reshape(rows, chan_width)

    def shape(dims, dtype=F32):
        return jax.ShapeDtypeStruct(dims, dtype)

    smem = pl.BlockSpec(memory_space=pltpu.SMEM)
    whole = pl.BlockSpec(memory_space=pltpu.VMEM)

    def call(kernel, scalars, arrays, outs, scratch=(), flops=0, size_bytes=0, specs=None):
        return pl.pallas_call(
            kernel,
            in_specs=[smem] * len(scalars) + (specs or [whole] * len(arrays)),
            out_shape=outs,
            scratch_shapes=[
                pltpu.VMEM(*entry) if isinstance(entry, tuple) else entry for entry in scratch
            ],
            compiler_params=params(),
            cost_estimate=cost(flops, size_bytes),
        )(*scalars, *arrays)

    half_x = shape((rows, half), BF16)
    half_w = shape((heads, size, size), BF16)
    half_v = shape((8, half))
    square, x_keep, x_send, upstream, w_keep, w_send, v_keep, v_send, opened = call(
        functools.partial(prepare_kernel, micro, tok_rows),
        [section_at, seq_at],
        [
            pltpu.with_memory_space_constraint(array, pltpu.HBM)
            for array in (
                doc_starts, x_raw, up_raw, rate_weight[0], input_weight[0],
                rate_bias, input_bias, decay_param, norm_gain,
            )
        ],
        [shape((8, rows)), half_x, half_x, half_x, half_w, half_w, half_v, half_v, shape((rows, 128))],
        [
            (doc_starts.shape, jnp.int32),
            ((rows, chan_width), BF16),
            ((rows, half), BF16),
            ((4, 1, chan_width), F32),
            pltpu.SemaphoreType.DMA((11,)),
        ],
        specs=[pl.BlockSpec(memory_space=pltpu.HBM)] * 9,
        flops=4 * rows * rows * chan_width,
        size_bytes=12 * rows * chan_width,
    )
    own_squares = chan_parts(square)
    other_squares = swap_sections(add_units(*own_squares))
    x_got, w_got, v_got = (swap_sections(value) for value in (x_send, w_send, v_send))

    big = shape((rows, half))
    blocks = shape((micro * 8, half))

    def forward(layer, beside):
        return call(
            functools.partial(
                forward_kernel, micro, tok_rows, full_width, layer, len(own_squares)
            ),
            [seq_at, section_at],
            [
                *own_squares, other_squares, opened, x_keep, x_got, w_keep, w_got, v_keep, v_got,
                beside,
            ],
            [
                half_x,
                shape((5, rows, half)),
                shape((3, micro * 8, half)),
                shape(((2 + layer) * micro, half)),
                shape((rows, 128)),
            ]
            + [blocks] * layer,
            [((rows, size), F32)] * 2,
            flops=4 * rows * size * half,
            size_bytes=24 * rows * half,
        )

    direct = seq_count == DIRECT_RANKS and heads == DIRECT_RANKS
    unit_dims = {0: [()] * 4, 1: [(2,)] * 2} if direct else {0: [(heads,)], 1: [(heads,)]}

    def backward(layer, pays, upstream, kept, rgrad, before):
        normed, factors, block, _, inv = kept
        return call(
            functools.partial(
                backward_kernel, micro, tok_rows, seq_count, layer, direct, len(pays)
            ),
            [seq_at, section_at],
            [
                *pays, x_keep, x_got, upstream, normed, factors, block, rgrad, inv,
                v_keep, v_got, w_keep, w_got, before,
            ],
            [big, shape((8, rows))]
            + [shape(dims + (size + VECTOR_ROWS, size), BF16) for dims in unit_dims[layer]],
            [
                ((micro, half), F32),
                ((micro, half), F32),
                ((tok_rows, size), F32),
                ((rows, size), F32),
                ((rows, size), BF16),
                ((rows, size), BF16),
                ((rows, 128), F32),
                ((heads, size + VECTOR_ROWS, size), BF16),
            ],
            flops=8 * rows * size * half,
            size_bytes=30 * rows * half,
        )

    def chip_sum(value):
        return add_units(value, swap_sections(value))

    *top, top_rgrad = forward(1, upstream)
    pays = seq_pays(top[3], seq_at, micro)
    low = forward(0, top[1])
    part, cross, *top_parts = backward(1, pays, upstream, top, top_rgrad, low[3])
    cross = chip_sum(cross)
    parts = chan_parts(cross)
    if direct:
        arrived = xor_moves(top_parts[1], "seq", 1)
    early, low_rgrad, low_pay = call(
        functools.partial(late_kernel, micro, tok_rows, full_width, len(parts)),
        [seq_at, section_at],
        [part, x_keep, x_got, top[4], low[1], low[3], *parts],
        [half_x, blocks, shape((3 * micro, half))],
        [((rows, 128), F32)],
        flops=8 * rows * half,
        size_bytes=12 * rows * half,
    )
    pays = seq_pays(low_pay, seq_at, micro)
    if direct:
        own_pair, far_pair = add_pairs(top_parts[0], after(arrived, pays[0]))
        arrived = xor_moves(far_pair, "seq", 2)
        top_own = add_units(own_pair, after(arrived, *pays))
        top_far = xor_moves(top_own, "seq", 2)
    part, cross, *low_parts = backward(
        0, pays, early, low, low_rgrad, top_own if direct else low_pay
    )
    sw = swap_sections(cross)
    cross = add_units(cross, after(sw, top_far) if direct else sw)
    parts = chan_parts(cross)
    if direct:
        place = lax.axis_index("seq")
        low_arrived = [xor_moves(low_parts[k], "seq", k) for k in (2, 1, 3)]
        low_arrived, parts = lax.optimization_barrier((low_arrived, parts))
        low_own = add_units(low_parts[0], *low_arrived)
        low_units = [low_own] + [xor_moves(low_own, "seq", k) for k in (1, 2, 3)]
        top_near = xor_moves(after(top_own, cross), "seq", 1)
        top_last = xor_moves(top_far, "seq", 1)
        top_units = [top_own, top_near, top_far, top_last]
    else:
        place = jnp.zeros((), jnp.int32)
        top_units, low_units = (
            [total[k] for k in range(heads)]
            for total in (
                lax.psum(value.astype(F32), "seq").astype(BF16)
                for value in (top_parts[0], low_parts[0])
            )
        )
    grads_keep, grads_send = call(
        functools.partial(last_kernel, full_width, tok_rows, len(parts)),
        [section_at],
        [part, x_keep, x_got, low[4], early, *parts],
        [half_x, half_x],
        flops=4 * rows * rows * half,
        size_bytes=12 * rows * half,
    )
    grads = call(
        join_kernel, [section_at], [grads_keep, swap_sections(grads_send)],
        shape((rows, chan_width), BF16), size_bytes=4 * rows * chan_width,
    )

    other_units = [
        swap_sections(jnp.where(section == 1, b, a)) for a, b in zip(top_units, low_units)
    ]
    rate_total, input_total, vector = pl.pallas_call(
        functools.partial(weights_kernel, heads, grad_scale),
        in_specs=[smem, smem] + [whole] * (3 * heads),
        out_specs=[pl.BlockSpec(memory_space=pltpu.HBM)] * 3,
        out_shape=[
            shape((heads, size, size)),
            shape((heads, size, size)),
            shape((3, 1, chan_width)),
        ],
        scratch_shapes=[
            pltpu.VMEM((2 * heads, size + VECTOR_ROWS, size), BF16),
            pltpu.VMEM((2 * heads, size, size), F32),
            pltpu.VMEM((3, 1, chan_width), F32),
            pltpu.SemaphoreType.DMA((2 * heads + 1,)),
        ],
        compiler_params=params(),
        cost_estimate=cost(0, 8 * heads * size * size),
    )(
        section_at, place.reshape(1).astype(jnp.int32), *top_units, *low_units, *other_units
    )
    return (
        grads.reshape(1, micro, tok_rows, chan_width),
        rate_total[None],
        input_total[None],
        jnp.swapaxes(vector, 0, 1),
    )


def solution(mesh):
    in_specs = (
        P("section", None, "seq", "chan"),
        P(None, "seq", "chan"),
        P("section", "chan", None, None),
        P("section", "chan", None, None),
        P("section", "chan"),
        P("section", "chan"),
        P("section", "chan"),
        P("section", "chan"),
        P(),
    )
    out_specs = (
        P("section", None, "seq", "chan"),
        P("section", "chan", None, None),
        P("section", "chan", None, None),
        P("section", None, "chan"),
    )
    return jax.shard_map(
        on_device, mesh=mesh, in_specs=in_specs, out_specs=out_specs, check_vma=False
    )
```
